256 devices in a mesh: frame: 4 (over z_lo, core), lat: 16 (over z_hi, y), lon: 4 (over x).
Axes of the slice: x: 4, y: 4, z: 8 (z_hi: 4, z_lo: 2; z = z_hi * 2 + z_lo), core: 2. Of those that a mesh axis runs over, the one named last changes fastest.
Arguments:
- latent_state: bfloat16 [8, 192, 64, 1024], P('frame', 'lat', 'lon'), may hold values from -6 to 6
- noise_draws: bfloat16 [1, 8, 192, 64, 1024], P(None, 'frame', 'lat', 'lon'), may hold values from -6 to 6
- step_index: int32 [8], P('frame'), may hold values from 0 to 5
- keep_frame: int32 [8], replicated, may hold values 0 or 1
- qkv_weight: bfloat16 [1024, 3072], P(('lat', 'lon')), may hold values from -0.1875 to 0.1875
- out_weight: bfloat16 [1024, 1024], P(('lat', 'lon')), may hold values from -0.1875 to 0.1875
Outputs:
- denoised: bfloat16 [8, 192, 64, 1024], P('frame', 'lat', 'lon')
The draws below stay inside these ranges and needn't reach their ends.
All inputs are finite; a program needn't handle non-finite values.
Results may differ from the reference program's by a relative error of at most 0.0038.
Values may be sent and summed in bfloat16 or wider, within the bound.
No kernel may reach another device: no remote copies, remote signals or barrier semaphores. Data moves between devices by JAX's collectives and lax.ppermute only.
A program may use at most 128 MiB of HBM per device.

```python
import math
import jax
import jax.numpy as jnp
from jax import lax

HEADS = 16
HEAD_DIM = 64
D = 1024
STEPS = 1
FRAMES = 8
NLAT = 192
NLON = 64


def set_ends(array, rng, low, largest):
    longest = array.shape.index(max(array.shape))
    spots = []
    for shift in (0, 1):
        where = [jax.random.randint(jax.random.fold_in(rng, axis), (), 0, length) for axis, length in enumerate(array.shape)]
        where[longest] = (where[longest] + shift) % array.shape[longest]
        spots.append(tuple(where))
    return array.at[spots[0]].set(low).at[spots[1]].set(largest)


def shard_levels(stream_key, dims, split, smallest, largest):
    def one(dim, blocks):
        heights = jax.random.uniform(jax.random.fold_in(jax.random.fold_in(stream_key, 6), dim), (blocks,), jnp.float32, smallest / len(split), largest / len(split))
        return jnp.repeat(jnp.exp(heights), dims[dim] // blocks).reshape((-1,) + (1,) * (len(dims) - dim - 1))

    loudness = one(*split[0])
    for cut in split[1:]:
        loudness = loudness * one(*cut)
    return loudness


def noise(key, shape, width, limit, pieces=(), kind=jnp.bfloat16):
    factor_of = shard_levels(key, shape, pieces, -0.22, 0.18) if pieces else 1.0
    array = jax.random.normal(key, shape, jnp.float32) * width * factor_of
    return jnp.minimum(jnp.maximum(array, -limit), limit).astype(kind)


def setup_inputs(seed: int = 0) -> dict:
    keys = jax.random.split(jax.random.key(seed), 7)
    return {
        "latent_state": noise(keys[0], (FRAMES, NLAT, NLON, D), 1.0, 6.0, ((0, 4), (1, 16), (2, 4))),
        "noise_draws": noise(keys[1], (STEPS, FRAMES, NLAT, NLON, D), 1.0, 6.0, ((1, 4), (2, 16), (3, 4))),
        "step_index": set_ends(jax.random.randint(keys[2], (FRAMES,), 0, 6), jax.random.fold_in(keys[2], 1), 0, 5).astype(jnp.int32),
        "keep_frame": set_ends((jax.random.randint(keys[3], (FRAMES,), 0, 3) < 2).astype(jnp.int32), jax.random.fold_in(keys[3], 1), 0, 1),
        "qkv_weight": noise(keys[4], (D, 3 * D), D ** -0.5, 0.1875, ((0, 64),)),
        "out_weight": noise(keys[5], (D, D), D ** -0.5, 0.1875, ((0, 64),)),
    }


window_reach = 6
sigma_top = 4.0
log_decay = math.log(0.8)
noise_share = 0.5

def sigma_of(levels):
    return sigma_top * jnp.exp(levels.astype(jnp.float32) * log_decay)

def rms_scale(values_in, epsilon):
    return values_in * lax.rsqrt(lax.optimization_barrier(jnp.mean(values_in * values_in, axis=-1, keepdims=True)) + epsilon)

def near_frame(operands):
    query_heads, key_heads, value_heads = operands
    window_side = 2 * window_reach + 1
    score_scale = HEAD_DIM ** (-0.5)
    anchor = jnp.int32(0)

    def widen(source):
        wrapped = jnp.concatenate([source[:, -window_reach:], source, source[:, :window_reach]], axis=1)
        return jnp.pad(wrapped.astype(jnp.float32), ((window_reach, window_reach), (0, 0), (0, 0), (0, 0)))
    key_pad = widen(key_heads)
    value_pad = widen(value_heads)
    query_full = query_heads.astype(jnp.float32)
    lat_rows = jnp.arange(NLAT + 2 * window_reach, dtype=jnp.int32) - window_reach
    inside = ((lat_rows >= 0) & (lat_rows < NLAT)).astype(jnp.float32)

    def offsets(offset):
        return ((offset // window_side).astype(jnp.int32), (offset % window_side).astype(jnp.int32))

    def raw_weight(offset):
        lat_offset, lon_offset = offsets(offset)
        shifted = lax.dynamic_slice(key_pad, (lat_offset, lon_offset, anchor, anchor), (NLAT, NLON, HEADS, HEAD_DIM))
        scores = lax.optimization_barrier(jnp.sum(query_full * shifted, axis=-1)) * score_scale
        lat_inside = lax.dynamic_slice(inside, (lat_offset,), (NLAT,))
        return jnp.exp(scores) * lat_inside[:, None, None]
    raw_weights = lax.map(raw_weight, jnp.arange(window_side * window_side, dtype=jnp.int32))
    denominator = lax.optimization_barrier(jnp.sum(raw_weights, axis=0))

    def accumulate(offset, running):
        lat_offset, lon_offset = offsets(offset)
        shifted = lax.dynamic_slice(value_pad, (lat_offset, lon_offset, anchor, anchor), (NLAT, NLON, HEADS, HEAD_DIM))
        weights = lax.optimization_barrier((raw_weights[offset] / denominator).astype(jnp.bfloat16))
        return running + weights.astype(jnp.float32)[..., None] * shifted
    return lax.fori_loop(0, window_side * window_side, accumulate, jnp.zeros((NLAT, NLON, HEADS, HEAD_DIM), jnp.float32))

def far_attention(query_heads, key_heads, value_heads, keep_frame):
    frame_ids = jnp.arange(FRAMES, dtype=jnp.int32)
    query_frame = frame_ids[:, None]
    key_frame = frame_ids[None, :]
    allowed = (key_frame == query_frame) | (key_frame < query_frame) & (keep_frame[None, :] == 1)
    scores = jnp.einsum('fxyhd,gxyhd->fgxyh', query_heads.astype(jnp.float32), key_heads.astype(jnp.float32), precision=lax.Precision.HIGHEST) * HEAD_DIM ** (-0.5)
    raw_weights = jnp.where(allowed[:, :, None, None, None], jnp.exp(scores), jnp.float32(0.0))
    weights = lax.optimization_barrier((raw_weights / lax.optimization_barrier(jnp.sum(raw_weights, axis=1, keepdims=True))).astype(jnp.bfloat16))
    return jnp.einsum('fgxyh,gxyhd->fxyhd', weights.astype(jnp.float32), value_heads.astype(jnp.float32), precision=lax.Precision.HIGHEST)

def reference(latent_state, noise_draws, step_index, keep_frame, qkv_weight, out_weight):
    current_state = latent_state
    for step_number in range(STEPS):
        current = current_state.astype(jnp.float32)
        normed = rms_scale(current, 1e-05).astype(jnp.bfloat16)
        projected = jnp.dot(normed.reshape(-1, D), qkv_weight, preferred_element_type=jnp.float32)
        projected = projected.reshape(FRAMES, NLAT, NLON, 3, HEADS, HEAD_DIM)
        query_heads = lax.optimization_barrier(rms_scale(projected[..., 0, :, :], 1e-06).astype(jnp.bfloat16))
        key_heads = lax.optimization_barrier(rms_scale(projected[..., 1, :, :], 1e-06).astype(jnp.bfloat16))
        value_heads = lax.optimization_barrier(projected[..., 2, :, :].astype(jnp.bfloat16))
        near_out = lax.map(near_frame, (query_heads, key_heads, value_heads))
        far_out = far_attention(query_heads, key_heads, value_heads, keep_frame)
        mixed_heads = (near_out + far_out).astype(jnp.bfloat16).reshape(-1, D)
        update = jnp.dot(mixed_heads, out_weight, preferred_element_type=jnp.float32).reshape(current.shape)
        levels = step_index + step_number
        noise_now = sigma_of(levels)
        noise_next = sigma_of(levels + 1)
        spread = noise_share * jnp.sqrt(noise_now * noise_now - noise_next * noise_next)
        current_state = (current + (noise_next - noise_now)[:, None, None, None] * update + spread[:, None, None, None] * noise_draws[step_number].astype(jnp.float32)).astype(jnp.bfloat16)
    return current_state
```

```python
import math

import jax
import jax.numpy as jnp
from jax import lax
from jax.experimental import pallas as pl
from jax.experimental.pallas import tpu as pltpu
from jax.sharding import PartitionSpec as P

HEAD_DIM = 64
REACH = 6
SIDE = 2 * REACH
SIGMA_TOP = 4.0
LOG_DECAY = math.log(0.8)
NOISE_SHARE = 0.5

FRAMES_DEV = 2
ROWS = 12
COLS = 16
CELLS = ROWS * COLS
WIDTH = 1024
TOTAL_ROWS = 192
FRAMES = 8
QUARTER = CELLS // 4
HALF = WIDTH // 2
QUAD = 256
KEYS = (ROWS + SIDE) * (COLS + SIDE)
NEAR_ROWS = FRAMES_DEV * KEYS
FAR_ROWS = FRAMES * QUARTER
OWN_ROWS = FRAMES_DEV * CELLS
VMEM = 50 * 1024 * 1024
BF16 = jnp.bfloat16
F32 = jnp.float32
EVERY = ("frame", "lat", "lon")


def place(z_lo, core, z_hi, y, x):
    return ((z_lo * 2 + core) * 16 + (z_hi % 4) * 4 + y % 4) * 4 + x % 4


def all_places():
    return [
        (z_lo, core, z_hi, y, x)
        for z_lo in range(2)
        for core in range(2)
        for z_hi in range(4)
        for y in range(4)
        for x in range(4)
    ]


def z_routes(slot):
    pairs = []
    for z_lo, core, z_hi, y, x in all_places():
        if slot == 1:
            source = (1 - z_lo, core, z_hi - 1 if z_lo == 0 else z_hi + 1, y, x)
        elif slot == 2:
            source = (z_lo, core, z_hi + 1 if z_lo == 0 else z_hi - 1, y, x)
        else:
            source = (1 - z_lo, core, z_hi + 2, y, x)
        pairs.append((place(*source), place(z_lo, core, z_hi, y, x)))
    return pairs


def plane_routes(stage, hop):
    pairs = []
    for z_lo, core, z_hi, y, x in all_places():
        along_y = (core == 0) == (stage == 2)
        target = (z_lo, core, z_hi, y + hop, x) if along_y else (z_lo, core, z_hi, y, x + hop)
        pairs.append((place(z_lo, core, z_hi, y, x), place(*target)))
    return pairs


def core_routes():
    return [(place(zl, c, zh, y, x), place(zl, 1 - c, zh, y, x)) for zl, c, zh, y, x in all_places()]


def frame_routes(hop):
    return [(p, (p + hop) % 4) for p in range(4)]


def row_order(half, z_lo, z_hi, y, x):
    spot = jnp.arange(WIDTH, dtype=jnp.int32)
    d3, d2, dz, k = spot // 256, (spot // 64) % 4, (spot // 16) % 4, spot % 16
    step = jnp.where(dz == 1, -1, jnp.where(dz == 2, 1, jnp.where(dz == 3, 2, 0)))
    step = jnp.where((z_lo == 1) & (dz < 3), -step, step)
    row_z = (z_hi + step) % 4
    first, last = (y - d2) % 4, (x - d3) % 4
    other_first, other_last = (x - d2) % 4, (y - d3) % 4
    row_y = jnp.where(half == 0, first, other_last)
    row_x = jnp.where(half == 0, last, other_first)
    return (row_z * 256 + row_y * 64 + row_x * 16 + k).reshape(1, WIDTH)


def near_mask(lat):
    spot = jnp.arange(KEYS, dtype=jnp.int32)
    own, top, bottom = CELLS, CELLS + 96, CELLS + 192
    side = spot - bottom
    side = jnp.where(side >= 144, side - 144, side)
    key_row = jnp.where(
        spot < own,
        REACH + spot // COLS,
        jnp.where(
            spot < top,
            (spot - own) // COLS,
            jnp.where(spot < bottom, ROWS + REACH + (spot - top) // COLS, side // REACH),
        ),
    )
    key_col = jnp.where(
        spot < bottom,
        REACH + spot % COLS,
        jnp.where(spot < bottom + 144, 0, COLS + REACH) + side % REACH,
    )
    cell = jnp.arange(CELLS, dtype=jnp.int32)
    lat_gap = key_row[None, :] - (cell // COLS)[:, None]
    lon_gap = key_col[None, :] - (cell % COLS)[:, None]
    global_row = lat * ROWS + key_row - REACH
    inside = (global_row >= 0) & (global_row < TOTAL_ROWS)
    seen = (lat_gap >= 0) & (lat_gap <= SIDE) & (lon_gap >= 0) & (lon_gap <= SIDE)
    return (seen & inside[None, :]).astype(BF16)


def shuffle_matrix(order_ref):
    rows = lax.broadcasted_iota(jnp.int32, (WIDTH, WIDTH), 0)
    return jnp.where(rows == order_ref[...], 1.0, 0.0).astype(BF16)


def prep_kernel(
    frame_ref, own, top, bottom, left, right, f0, f1, f2, f3, order_a, order_b,
    near_a, near_b, far_a, far_b, near_tmp, far_tmp, mix_a, mix_b,
):
    mix_a[...] = shuffle_matrix(order_a)
    mix_b[...] = shuffle_matrix(order_b)

    def norm(source, start, target, offset, count, chunk):
        def step(index, carry):
            rows = source[pl.ds(pl.multiple_of(start + index * chunk, 16), chunk), :].astype(F32)
            scale = lax.rsqrt(jnp.mean(rows * rows, axis=-1, keepdims=True) + 1e-05)
            target[pl.ds(pl.multiple_of(offset + index * chunk, 16), chunk), :] = (rows * scale).astype(BF16)
            return carry

        lax.fori_loop(0, count // chunk, step, 0)

    for f in range(FRAMES_DEV):
        base = f * KEYS
        norm(own, f * CELLS, near_tmp, base, CELLS, 48)
        norm(top, f * 96, near_tmp, base + CELLS, 96, 48)
        norm(bottom, f * 96, near_tmp, base + CELLS + 96, 96, 48)
        norm(left, f * 144, near_tmp, base + CELLS + 192, 144, 48)
        norm(right, f * 144, near_tmp, base + CELLS + 336, 144, 48)
    for hop, piece in enumerate((f0, f1, f2, f3)):
        source = lax.rem(frame_ref[0] + 4 - hop, 4)
        norm(piece, 0, far_tmp, source * (2 * QUARTER), 2 * QUARTER, 48)

    def near_step(index, carry):
        rows = pl.ds(pl.multiple_of(index * 96, 96), 96)
        block = near_tmp[rows, :]
        near_a[rows, :] = jnp.dot(block, mix_a[...], preferred_element_type=F32).astype(BF16)
        near_b[rows, :] = jnp.dot(block, mix_b[...], preferred_element_type=F32).astype(BF16)
        return carry

    lax.fori_loop(0, NEAR_ROWS // 96, near_step, 0)

    def far_step(index, carry):
        rows = pl.ds(pl.multiple_of(index * 96, 96), 96)
        block = far_tmp[rows, :]
        far_a[rows, :] = jnp.dot(block, mix_a[...], preferred_element_type=F32).astype(BF16)
        far_b[rows, :] = jnp.dot(block, mix_b[...], preferred_element_type=F32).astype(BF16)
        return carry

    lax.fori_loop(0, FAR_ROWS // 96, far_step, 0)


def prepare(frame, own, top, bottom, left, right, far, order_a, order_b):
    whole = pl.BlockSpec(memory_space=pltpu.VMEM)
    return pl.pallas_call(
        prep_kernel,
        out_shape=[
            jax.ShapeDtypeStruct((NEAR_ROWS, WIDTH), BF16),
            jax.ShapeDtypeStruct((NEAR_ROWS, WIDTH), BF16),
            jax.ShapeDtypeStruct((FAR_ROWS, WIDTH), BF16),
            jax.ShapeDtypeStruct((FAR_ROWS, WIDTH), BF16),
        ],
        in_specs=[pl.BlockSpec(memory_space=pltpu.SMEM)] + [whole] * 11,
        out_specs=[whole] * 4,
        scratch_shapes=[
            pltpu.VMEM((NEAR_ROWS, WIDTH), BF16),
            pltpu.VMEM((FAR_ROWS, WIDTH), BF16),
            pltpu.VMEM((WIDTH, WIDTH), BF16),
            pltpu.VMEM((WIDTH, WIDTH), BF16),
        ],
        compiler_params=pltpu.CompilerParams(vmem_limit_bytes=VMEM),
        cost_estimate=pl.CostEstimate(flops=8 * 10**9, bytes_accessed=11 * 10**6, transcendentals=0),
        name="prep",
    )(frame, own, top, bottom, left, right, *far, order_a, order_b)


def project(rows, pieces):
    total = jnp.dot(rows[:, :256], pieces[0][...], preferred_element_type=F32)
    for d in range(1, 4):
        total += jnp.dot(rows[:, d * 256 : (d + 1) * 256], pieces[d][...], preferred_element_type=F32)
    return total


def head_ones():
    row = lax.broadcasted_iota(jnp.int32, (QUAD, QUAD), 0) // HEAD_DIM
    col = lax.broadcasted_iota(jnp.int32, (QUAD, QUAD), 1) // HEAD_DIM
    return jnp.where(row == col, 1.0, 0.0).astype(BF16)


def head_scale(values, ones):
    squares = jnp.dot((values * values).astype(BF16), ones, preferred_element_type=F32)
    return values * lax.rsqrt(squares * (1.0 / HEAD_DIM) + 1e-06)


def near_kernel(*refs):
    rows_ref, mask_ref = refs[:2]
    wq, wk, wv = refs[2:6], refs[6:10], refs[10:14]
    out_ref, queries, keys, values = refs[14:]
    ones = head_ones()

    def key_step(index, carry):
        spot = pl.ds(pl.multiple_of(index * 192, 192), 192)
        block = rows_ref[spot, :]
        keys[spot, :] = head_scale(project(block, wk), ones).astype(BF16)
        found = project(block, wv).astype(BF16)
        values[spot, :128] = found[:, :128]
        values[spot, 128:256] = jnp.ones((192, 128), BF16)
        values[spot, 256:384] = found[:, 128:]
        values[spot, 384:] = jnp.ones((192, 128), BF16)
        return carry

    lax.fori_loop(0, NEAR_ROWS // 192, key_step, 0)
    for f in range(FRAMES_DEV):
        found = head_scale(project(rows_ref[f * KEYS : f * KEYS + CELLS, :], wq), ones).astype(BF16)
        queries[f * CELLS : (f + 1) * CELLS, :] = found * jnp.bfloat16(0.125)

    lane = lax.broadcasted_iota(jnp.int32, (CELLS, 128), 1)

    def attend(index, carry):
        f, pair = index // 2, index % 2
        cells = pl.ds(pl.multiple_of(f * CELLS, CELLS), CELLS)
        spots = pl.ds(pl.multiple_of(f * KEYS, 96), KEYS)
        lanes = pl.ds(pl.multiple_of(pair * 128, 128), 128)
        query = queries[cells, lanes]
        key = keys[spots, lanes]
        value = values[spots, pl.ds(pl.multiple_of(pair * 256, 256), 256)]
        parts = []
        for member in range(2):
            chosen = jnp.where((lane < HEAD_DIM) == (member == 0), query, jnp.bfloat16(0.0))
            scores = lax.dot_general(chosen, key, (((1,), (1,)), ((), ())), preferred_element_type=F32)
            weights = jnp.exp(scores).astype(BF16) * mask_ref[...]
            found = jnp.dot(weights, value, preferred_element_type=F32)
            parts.append(found[:, :128] / found[:, 128:])
        out_ref[cells, lanes] = jnp.where(lane < HEAD_DIM, parts[0], parts[1])
        return carry

    lax.fori_loop(0, 4, attend, 0)


def weight_specs():
    specs = []
    for part in range(3):
        for _ in range(4):
            specs.append(pl.BlockSpec((256, QUAD), lambda j, part=part: (0, part * 2 + j)))
    return specs


def near_half(rows, mask, pieces):
    return pl.pallas_call(
        near_kernel,
        grid=(2,),
        out_shape=jax.ShapeDtypeStruct((OWN_ROWS, HALF), F32),
        in_specs=[
            pl.BlockSpec((NEAR_ROWS, WIDTH), lambda j: (0, 0)),
            pl.BlockSpec((CELLS, KEYS), lambda j: (0, 0)),
        ]
        + weight_specs(),
        out_specs=pl.BlockSpec((OWN_ROWS, QUAD), lambda j: (0, j)),
        scratch_shapes=[
            pltpu.VMEM((OWN_ROWS, QUAD), BF16),
            pltpu.VMEM((NEAR_ROWS, QUAD), BF16),
            pltpu.VMEM((NEAR_ROWS, 2 * QUAD), BF16),
        ],
        compiler_params=pltpu.CompilerParams(vmem_limit_bytes=VMEM),
        cost_estimate=pl.CostEstimate(flops=8 * 10**9, bytes_accessed=7 * 10**6, transcendentals=2 * 10**6),
        name="near",
    )(rows, mask, *pieces, *pieces, *pieces)


def far_kernel(*refs):
    keep_ref, rows_ref = refs[:2]
    wq, wk, wv = refs[2:6], refs[6:10], refs[10:14]
    out_ref, queries, keys, values = refs[14:]
    ones = head_ones()

    def step(index, carry):
        spot = pl.ds(pl.multiple_of(index * 192, 192), 192)
        block = rows_ref[spot, :]
        found = head_scale(project(block, wq), ones).astype(BF16)
        queries[spot, :] = found * jnp.bfloat16(0.125)
        keys[spot, :] = head_scale(project(block, wk), ones).astype(BF16)
        values[spot, :] = project(block, wv).astype(BF16)
        return carry

    lax.fori_loop(0, FAR_ROWS // 192, step, 0)
    for f in range(FRAMES):
        query = queries[f * QUARTER : (f + 1) * QUARTER, :]
        products = [query * keys[g * QUARTER : (g + 1) * QUARTER, :] for g in range(f + 1)]
        scores = jnp.dot(jnp.concatenate(products, axis=0), ones, preferred_element_type=F32)
        raw = jnp.exp(scores)
        total = raw[f * QUARTER :, :]
        mixed = total * values[f * QUARTER : (f + 1) * QUARTER, :].astype(F32)
        for g in range(f):
            kept = jnp.where(keep_ref[g] == 1, 1.0, 0.0).astype(F32)
            weight = raw[g * QUARTER : (g + 1) * QUARTER, :] * kept
            total += weight
            mixed += weight * values[g * QUARTER : (g + 1) * QUARTER, :].astype(F32)
        out_ref[f * QUARTER : (f + 1) * QUARTER, :] = (mixed / total).astype(BF16)


def far_half(keep, rows, pieces):
    return pl.pallas_call(
        far_kernel,
        grid=(2,),
        out_shape=jax.ShapeDtypeStruct((FAR_ROWS, HALF), BF16),
        in_specs=[
            pl.BlockSpec(memory_space=pltpu.SMEM),
            pl.BlockSpec((FAR_ROWS, WIDTH), lambda j: (0, 0)),
        ]
        + weight_specs(),
        out_specs=pl.BlockSpec((FAR_ROWS, QUAD), lambda j: (0, j)),
        scratch_shapes=[pltpu.VMEM((FAR_ROWS, QUAD), BF16)] * 3,
        compiler_params=pltpu.CompilerParams(vmem_limit_bytes=VMEM),
        cost_estimate=pl.CostEstimate(flops=2 * 10**9, bytes_accessed=5 * 10**6, transcendentals=10**6),
        name="far",
    )(keep, rows, *pieces, *pieces, *pieces)


def out_kernel(*refs):
    place_ref, coef_ref, near_a, near_b = refs[:4]
    far_same, far_swap = (refs[4], refs[6]), (refs[5], refs[7])
    weights_a, weights_b = refs[8:12], refs[12:16]
    order_a, order_b, state_ref, noise_ref, out_ref, mixed, update = refs[16:]
    frame = place_ref[0]
    core = lax.rem(frame, 2)
    lanes_a = pl.ds(pl.multiple_of(core * HALF, HALF), HALF)
    lanes_b = pl.ds(pl.multiple_of((1 - core) * HALF, HALF), HALF)
    for hop in range(4):
        piece = (far_same if hop % 2 == 0 else far_swap)[hop // 2]
        source = lax.rem(frame + 4 - hop, 4)
        for f in range(FRAMES_DEV):
            cells = pl.ds(pl.multiple_of(f * CELLS + source * QUARTER, QUARTER), QUARTER)
            arrived = slice(f * QUARTER, (f + 1) * QUARTER)
            first, second = piece[arrived, :HALF], piece[arrived, HALF:]
            if hop % 2 == 1:
                first, second = second, first
            mixed[cells, lanes_a] = (near_a[cells, :] + first.astype(F32)).astype(BF16)
            mixed[cells, lanes_b] = (near_b[cells, :] + second.astype(F32)).astype(BF16)
    for lanes, order, pieces in ((lanes_a, order_a, weights_a), (lanes_b, order_b, weights_b)):
        for chunk in range(2):
            rows = slice(chunk * CELLS, (chunk + 1) * CELLS)
            shuffled = jnp.dot(mixed[rows, :], shuffle_matrix(order), preferred_element_type=F32).astype(BF16)
            update[rows, lanes] = project(shuffled, pieces)
    for f in range(FRAMES_DEV):
        rows = slice(f * CELLS, (f + 1) * CELLS)
        out_ref[rows, :] = (
            state_ref[rows, :].astype(F32)
            + coef_ref[0, f] * update[rows, :]
            + coef_ref[1, f] * noise_ref[rows, :].astype(F32)
        ).astype(BF16)


def finish(place_ids, coefs, near_a, near_b, far, pieces_a, pieces_b, order_a, order_b, state, noise):
    whole = pl.BlockSpec(memory_space=pltpu.VMEM)
    scalar = pl.BlockSpec(memory_space=pltpu.SMEM)
    return pl.pallas_call(
        out_kernel,
        out_shape=jax.ShapeDtypeStruct((OWN_ROWS, WIDTH), BF16),
        in_specs=[scalar, scalar] + [whole] * 18,
        out_specs=whole,
        scratch_shapes=[pltpu.VMEM((OWN_ROWS, WIDTH), BF16), pltpu.VMEM((OWN_ROWS, WIDTH), F32)],
        compiler_params=pltpu.CompilerParams(vmem_limit_bytes=VMEM),
        cost_estimate=pl.CostEstimate(flops=3 * 10**9, bytes_accessed=7 * 10**6, transcendentals=0),
        name="out",
    )(place_ids, coefs, near_a, near_b, *far, *pieces_a, *pieces_b, order_a, order_b, state, noise)


def sigma_of(levels):
    return SIGMA_TOP * jnp.exp(levels.astype(F32) * LOG_DECAY)


def body(latent_state, noise_draws, step_index, keep_frame, qkv_weight, out_weight):
    frame = lax.axis_index("frame")
    lat = lax.axis_index("lat")
    x = lax.axis_index("lon")
    core, z_lo = frame % 2, frame // 2
    z_hi, y = lat // 4, lat % 4

    top = lax.ppermute(latent_state[:, ROWS - REACH :], "lat", [(i, i + 1) for i in range(15)])
    bottom = lax.ppermute(latent_state[:, :REACH], "lat", [(i + 1, i) for i in range(15)])
    columns = [lax.dynamic_slice(qkv_weight, (0, s * WIDTH + core * HALF), (16, HALF)) for s in range(3)]
    columns.append(lax.dynamic_slice(out_weight, (0, core * HALF), (16, HALF)))
    own_rows = jnp.concatenate(columns, axis=1)
    z_rows = jnp.concatenate(
        [own_rows] + [lax.ppermute(own_rows, EVERY, z_routes(slot)) for slot in (1, 2, 3)], axis=0
    )
    quarters = latent_state.reshape(FRAMES_DEV, 4, QUARTER, WIDTH)

    def quarter(index):
        taken = lax.dynamic_index_in_dim(quarters, index % 4, axis=1, keepdims=False)
        return taken.reshape(FRAMES_DEV * QUARTER, WIDTH)

    far_in = [quarter(frame)] + [
        lax.ppermute(quarter(frame + hop), "frame", frame_routes(hop)) for hop in (1, 2, 3)
    ]
    tall = jnp.concatenate([top, latent_state, bottom], axis=1)
    right_edge = tall[:, :, COLS - REACH :].reshape(-1, WIDTH)
    left_edge = tall[:, :, :REACH].reshape(-1, WIDTH)
    left = lax.ppermute(right_edge, "lon", [(i, (i + 1) % 4) for i in range(4)])
    right = lax.ppermute(left_edge, "lon", [((i + 1) % 4, i) for i in range(4)])
    plane = [z_rows] + [lax.ppermute(z_rows, EVERY, plane_routes(2, hop)) for hop in (1, 2, 3)]
    split = 3 * HALF
    qkv_rows = jnp.concatenate([part[:, :split] for part in plane], axis=0)
    out_rows = jnp.concatenate([part[:, split:] for part in plane], axis=0)
    qkv_a = [qkv_rows] + [lax.ppermute(qkv_rows, EVERY, plane_routes(3, hop)) for hop in (1, 3, 2)]
    qkv_a = [qkv_a[0], qkv_a[1], qkv_a[3], qkv_a[2]]
    qkv_b = [lax.ppermute(piece, EVERY, core_routes()) for piece in qkv_a]
    out_a = [out_rows] + [lax.ppermute(out_rows, EVERY, plane_routes(3, hop)) for hop in (1, 2, 3)]
    out_b = [lax.ppermute(piece, EVERY, core_routes()) for piece in out_a]

    order_a = row_order(core, z_lo, z_hi, y, x)
    order_b = row_order(1 - core, z_lo, z_hi, y, x)
    place_ids = frame.reshape(1).astype(jnp.int32)
    state = latent_state.reshape(OWN_ROWS, WIDTH)
    rows_a, rows_b, frames_a, frames_b = prepare(
        place_ids, state, top.reshape(-1, WIDTH), bottom.reshape(-1, WIDTH), left, right, far_in, order_a, order_b
    )
    mask = near_mask(lat)
    far_a = far_half(keep_frame, frames_a, qkv_a)
    near_a = near_half(rows_a, mask, qkv_a)
    far_b = far_half(keep_frame, frames_b, qkv_b)
    far_out = jnp.concatenate([far_a, far_b], axis=1).reshape(4, FRAMES_DEV * QUARTER, WIDTH)

    def frames_of(index):
        return lax.dynamic_index_in_dim(far_out, index % 4, axis=0, keepdims=False)

    far_back = [frames_of(frame)] + [
        lax.ppermute(frames_of(frame + hop), "frame", frame_routes(hop)) for hop in (1, 2, 3)
    ]
    near_b = near_half(rows_b, mask, qkv_b)

    noise_now = sigma_of(step_index)
    noise_next = sigma_of(step_index + 1)
    spread = NOISE_SHARE * jnp.sqrt(noise_now * noise_now - noise_next * noise_next)
    coefs = jnp.stack([noise_next - noise_now, spread])
    denoised = finish(
        place_ids, coefs, near_a, near_b, far_back, out_a, out_b, order_a, order_b,
        state, noise_draws.reshape(OWN_ROWS, WIDTH),
    )
    return denoised.reshape(latent_state.shape)


def solution(mesh):
    return jax.shard_map(
        body,
        mesh=mesh,
        in_specs=(
            P("frame", "lat", "lon", None),
            P(None, "frame", "lat", "lon", None),
            P("frame"),
            P(),
            P(("lat", "lon"), None),
            P(("lat", "lon"), None),
        ),
        out_specs=P("frame", "lat", "lon", None),
        check_vma=False,
    )
```

```python
import functools
import math

import jax
import jax.numpy as jnp
from jax import lax
from jax.experimental import pallas as pl
from jax.experimental.pallas import tpu as pltpu
from jax.sharding import PartitionSpec as P

HEAD_DIM = 64
REACH = 6
SIDE = 2 * REACH
SIGMA_TOP = 4.0
LOG_DECAY = math.log(0.8)
NOISE_SHARE = 0.5

FRAMES_DEV = 2
ROWS = 12
COLS = 16
CELLS = ROWS * COLS
WIDTH = 1024
TOTAL_ROWS = 192
FRAMES = 8
QUARTER = CELLS // 4
HALF = WIDTH // 2
QUAD = 256
MID = 176
LOW = MID + ROWS * (COLS + SIDE)
KEYS = LOW + 176
BAND = CELLS // 2
BAND_SKIP = MID
BAND_KEYS = LOW
NEAR_ROWS = FRAMES_DEV * KEYS
FAR_ROWS = FRAMES * QUARTER
OWN_ROWS = FRAMES_DEV * CELLS
VMEM = 32 * 1024 * 1024
BF16 = jnp.bfloat16
F32 = jnp.float32
EVERY = ("frame", "lat", "lon")


def place(z_lo, core, z_hi, y, x):
    return ((z_lo * 2 + core) * 16 + (z_hi % 4) * 4 + y % 4) * 4 + x % 4


def all_places():
    return [
        (z_lo, core, z_hi, y, x)
        for z_lo in range(2)
        for core in range(2)
        for z_hi in range(4)
        for y in range(4)
        for x in range(4)
    ]


def z_routes(slot):
    pairs = []
    for z_lo, core, z_hi, y, x in all_places():
        if slot == 1:
            source = (1 - z_lo, core, z_hi - 1 if z_lo == 0 else z_hi + 1, y, x)
        elif slot == 2:
            source = (z_lo, core, z_hi + 1 if z_lo == 0 else z_hi - 1, y, x)
        else:
            source = (1 - z_lo, core, z_hi + 2, y, x)
        pairs.append((place(*source), place(z_lo, core, z_hi, y, x)))
    return pairs


def plane_routes(stage, hop):
    pairs = []
    for z_lo, core, z_hi, y, x in all_places():
        along_y = (core == 0) == (stage == 2)
        target = (z_lo, core, z_hi, y + hop, x) if along_y else (z_lo, core, z_hi, y, x + hop)
        pairs.append((place(z_lo, core, z_hi, y, x), place(*target)))
    return pairs


def core_routes():
    return [(place(zl, c, zh, y, x), place(zl, 1 - c, zh, y, x)) for zl, c, zh, y, x in all_places()]


def frame_routes(hop):
    return [(p, (p + hop) % 4) for p in range(4)]


def place_kernel(mode, spots_ref, *refs):
    arrived, targets = refs[:4], refs[4:]
    split = 3 * HALF

    def run(by_first):
        for d in range(4):
            spot = spots_ref[d]
            if mode == 1:
                targets[0][spot] = arrived[d][...]
                continue

            def step(z, carry, d=d, spot=spot):
                if mode == 2:
                    targets[0][z, spot] = arrived[d][z, :, :split]
                    targets[1][z, spot] = arrived[d][z, :, split:]
                elif by_first:
                    targets[0][z, spot] = arrived[d][z]
                else:
                    targets[0][z, :, spot] = arrived[d][z]
                return carry

            lax.fori_loop(0, 4, step, 0)

    if mode < 3:
        run(False)
    else:
        pl.when(spots_ref[4] == 0)(lambda: run(False))
        pl.when(spots_ref[4] == 1)(lambda: run(True))


def place_rows(mode, spots, arrived, shapes):
    whole = pl.BlockSpec(memory_space=pltpu.VMEM)
    size = sum(2 * math.prod(shape) for shape in shapes)
    return pl.pallas_call(
        functools.partial(place_kernel, mode),
        out_shape=[jax.ShapeDtypeStruct(shape, BF16) for shape in shapes],
        in_specs=[pl.BlockSpec(memory_space=pltpu.SMEM)] + [whole] * 4,
        out_specs=[whole] * len(shapes),
        compiler_params=pltpu.CompilerParams(vmem_limit_bytes=VMEM),
        cost_estimate=pl.CostEstimate(flops=0, bytes_accessed=2 * size, transcendentals=0),
        name="place",
    )(spots, *arrived)


def near_mask(lat):
    spot = jnp.arange(BAND_KEYS, dtype=jnp.int32)[None, :]
    cell = jnp.arange(CELLS, dtype=jnp.int32)[:, None]
    spot = spot + jnp.where(cell < CELLS // 2, 0, BAND_SKIP)
    part = jnp.where(spot < MID, 0, jnp.where(spot < LOW, 1, 2))
    base = jnp.where(part == 0, 0, jnp.where(part == 1, MID, LOW))
    first_row = jnp.where(part == 0, 0, jnp.where(part == 1, REACH, REACH + ROWS))
    tall = jnp.where(part == 1, ROWS, REACH)
    local = spot - base
    centre = tall * COLS
    edge = tall * REACH
    side = local - centre
    right = side >= edge
    side = jnp.where(right, side - edge, side)
    inner = local < centre
    key_row = first_row + jnp.where(inner, local // COLS, side // REACH)
    key_col = jnp.where(
        inner, REACH + local % COLS, jnp.where(right, COLS + REACH, 0) + side % REACH
    )
    lat_gap = key_row - cell // COLS
    lon_gap = key_col - cell % COLS
    global_row = lat * ROWS + key_row - REACH
    inside = (global_row >= 0) & (global_row < TOTAL_ROWS) & (local < centre + 2 * edge)
    seen = (lat_gap >= 0) & (lat_gap <= SIDE) & (lon_gap >= 0) & (lon_gap <= SIDE)
    return (seen & inside).astype(BF16)


def edge_kernel(own, top, bottom, east, west, east_tmp, west_tmp):
    for f in range(FRAMES_DEV):
        for row in range(ROWS + SIDE):
            if row < REACH:
                block = top[f, row]
            elif row < REACH + ROWS:
                block = own[f, row - REACH]
            else:
                block = bottom[f, row - REACH - ROWS]
            block = block.astype(F32)
            start = (f * (ROWS + SIDE) + row) * REACH
            east_tmp[start : start + REACH, :] = block[COLS - REACH :]
            west_tmp[start : start + REACH, :] = block[:REACH]
    east[...] = east_tmp[...].astype(BF16)
    west[...] = west_tmp[...].astype(BF16)


def edges_of(own, top, bottom):
    whole = pl.BlockSpec(memory_space=pltpu.VMEM)
    rows = FRAMES_DEV * (ROWS + SIDE) * REACH
    return pl.pallas_call(
        edge_kernel,
        out_shape=[jax.ShapeDtypeStruct((rows, WIDTH), BF16)] * 2,
        in_specs=[whole] * 3,
        out_specs=[whole] * 2,
        scratch_shapes=[pltpu.VMEM((rows, WIDTH), F32)] * 2,
        compiler_params=pltpu.CompilerParams(vmem_limit_bytes=VMEM),
        cost_estimate=pl.CostEstimate(flops=10**6, bytes_accessed=3 * 10**6, transcendentals=0),
        name="edges",
    )(own, top, bottom)


def normed(block):
    rows = block.astype(F32)
    return rows * lax.rsqrt(jnp.mean(rows * rows, axis=-1, keepdims=True) + 1e-05)


def prep_kernel(own, top, bottom, left, right, near_out, rows_tmp, edge_tmp):
    def place_rows(source, start, offset, count):
        def step(index, carry):
            taken = source[pl.ds(pl.multiple_of(start + index * 48, 16), 48), :]
            rows_tmp[pl.ds(pl.multiple_of(offset + index * 48, 16), 48), :] = normed(taken)
            return carry

        lax.fori_loop(0, count // 48, step, 0)

    for f in range(FRAMES_DEV):
        base = f * KEYS
        place_rows(own, f * CELLS, base + MID, CELLS)
        place_rows(top, f * 96, base, 96)
        place_rows(bottom, f * 96, base + LOW, 96)
        rows_tmp[base + MID - 8 : base + MID, :] = jnp.zeros((8, WIDTH), F32)
        rows_tmp[base + KEYS - 8 : base + KEYS, :] = jnp.zeros((8, WIDTH), F32)
    for index, edge in enumerate((left, right)):
        for chunk in range(6):
            spot = slice(chunk * 48, (chunk + 1) * 48)
            edge_tmp[spot, :] = normed(edge[spot, :])
        for f in range(FRAMES_DEV):
            for first, count, target in (
                (0, 36, 96 + index * 36),
                (36, 72, MID + CELLS + index * 72),
                (108, 36, LOW + 96 + index * 36),
            ):
                start = f * 144 + first
                rows_tmp[f * KEYS + target : f * KEYS + target + count, :] = edge_tmp[start : start + count, :]

    def settle(index, carry):
        rows = pl.ds(pl.multiple_of(index * 32, 32), 32)
        near_out[rows, :] = rows_tmp[rows, :].astype(BF16)
        return carry

    lax.fori_loop(0, NEAR_ROWS // 32, settle, 0)

def far_prep_kernel(frame_ref, f0, f1, f2, f3, far_out):
    for hop, piece in enumerate((f0, f1, f2, f3)):
        source = lax.rem(frame_ref[0] + 4 - hop, 4)

        def far_step(index, carry, piece=piece, source=source):
            taken = piece[pl.ds(pl.multiple_of(index * 48, 16), 48), :]
            target = pl.ds(pl.multiple_of(source * (2 * QUARTER) + index * 48, 16), 48)
            far_out[target, :] = normed(taken).astype(BF16)
            return carry

        lax.fori_loop(0, 2, far_step, 0)


def prepare_far(frame, far):
    whole = pl.BlockSpec(memory_space=pltpu.VMEM)
    return pl.pallas_call(
        far_prep_kernel,
        out_shape=jax.ShapeDtypeStruct((FAR_ROWS, WIDTH), BF16),
        in_specs=[pl.BlockSpec(memory_space=pltpu.SMEM)] + [whole] * 4,
        out_specs=whole,
        compiler_params=pltpu.CompilerParams(vmem_limit_bytes=VMEM),
        cost_estimate=pl.CostEstimate(flops=10**8, bytes_accessed=16 * 10**5, transcendentals=0),
        name="prep_far",
    )(frame, *far)


def prepare(own, top, bottom, left, right):
    whole = pl.BlockSpec(memory_space=pltpu.VMEM)
    return pl.pallas_call(
        prep_kernel,
        out_shape=jax.ShapeDtypeStruct((NEAR_ROWS, WIDTH), BF16),
        in_specs=[whole] * 5,
        out_specs=whole,
        scratch_shapes=[pltpu.VMEM((NEAR_ROWS, WIDTH), F32), pltpu.VMEM((288, WIDTH), F32)],
        compiler_params=pltpu.CompilerParams(vmem_limit_bytes=VMEM),
        cost_estimate=pl.CostEstimate(flops=10**9, bytes_accessed=8 * 10**6, transcendentals=0),
        name="prep",
    )(own, top, bottom, left, right)


def head_ones():
    row = lax.broadcasted_iota(jnp.int32, (QUAD, QUAD), 0) // HEAD_DIM
    col = lax.broadcasted_iota(jnp.int32, (QUAD, QUAD), 1) // HEAD_DIM
    return jnp.where(row == col, 1.0, 0.0).astype(BF16)


def head_scale(values, ones):
    squares = jnp.dot((values * values).astype(BF16), ones, preferred_element_type=F32)
    return values * lax.rsqrt(squares * (1.0 / HEAD_DIM) + 1e-06)


def scaled_heads(rows, weights, part, ones, target, spot, factor):
    found = jnp.dot(rows, weights[:, part * HALF : (part + 1) * HALF], preferred_element_type=F32)
    for quad in range(2):
        lanes = slice(quad * QUAD, (quad + 1) * QUAD)
        target[spot, lanes] = head_scale(found[:, lanes], ones).astype(BF16) * jnp.bfloat16(factor)


def near_part(rows_ref, mask_ref, out_ref, weights, queries, keys, values, ones):
    def key_step(index, carry):
        spot = pl.ds(pl.multiple_of(index * KEYS, 16), KEYS)
        block = rows_ref[spot, :]
        scaled_heads(block, weights, 1, ones, keys, spot, 1.0)
        values[spot, :] = jnp.dot(block, weights[:, 2 * HALF :], preferred_element_type=F32).astype(BF16)
        cells = rows_ref[pl.ds(pl.multiple_of(index * KEYS + MID, 16), CELLS), :]
        target = pl.ds(pl.multiple_of(index * CELLS, CELLS), CELLS)
        scaled_heads(cells, weights, 0, ones, queries, target, HEAD_DIM**-0.5)
        return carry

    lax.fori_loop(0, FRAMES_DEV, key_step, 0)

    head = lax.broadcasted_iota(jnp.int32, (BAND, QUAD), 1) // HEAD_DIM

    def attend(f, quad, band):
        lanes = slice(quad * QUAD, (quad + 1) * QUAD)
        cells = pl.ds(pl.multiple_of(f * CELLS + band * BAND, BAND), BAND)
        spots = pl.ds(pl.multiple_of(f * KEYS + band * BAND_SKIP, 16), BAND_KEYS)
        query = queries[cells, lanes]
        stacked = jnp.concatenate(
            [jnp.where(head == member, query, jnp.bfloat16(0.0)) for member in range(4)], axis=0
        )
        scores = lax.dot_general(
            stacked, keys[spots, lanes], (((1,), (1,)), ((), ())), preferred_element_type=F32
        )
        seen = mask_ref[band * BAND : (band + 1) * BAND, :]
        raw = jnp.exp(scores).astype(BF16) * jnp.concatenate([seen] * 4, axis=0)
        found = jnp.dot(raw, values[spots, lanes], preferred_element_type=F32)
        found = found / jnp.sum(raw.astype(F32), axis=-1, keepdims=True)
        result = found[:BAND]
        for member in range(1, 4):
            result = jnp.where(head == member, found[member * BAND : (member + 1) * BAND], result)
        out_ref[cells, lanes] = result

    def step(f, carry):
        for quad in range(2):
            for band in range(2):
                attend(f, quad, band)
        return carry

    lax.fori_loop(0, FRAMES_DEV, step, 0)


def far_part(keep_ref, rows_ref, out_ref, weights, queries, keys, values, ones):
    block, every = rows_ref[...], slice(0, FAR_ROWS)
    scaled_heads(block, weights, 0, ones, queries, every, HEAD_DIM**-0.5)
    scaled_heads(block, weights, 1, ones, keys, every, 1.0)
    values[every, :] = jnp.dot(block, weights[:, 2 * HALF :], preferred_element_type=F32).astype(BF16)
    kept = [jnp.where(keep_ref[g] == 1, 1.0, 0.0).astype(F32) for g in range(FRAMES)]
    for quad in range(2):
        lanes = slice(quad * QUAD, (quad + 1) * QUAD)
        for f in range(FRAMES):
            query = queries[f * QUARTER : (f + 1) * QUARTER, lanes]
            products = [query * keys[g * QUARTER : (g + 1) * QUARTER, lanes] for g in range(f + 1)]
            scores = jnp.dot(jnp.concatenate(products, axis=0), ones, preferred_element_type=F32)
            raw = jnp.exp(scores)
            total = raw[f * QUARTER :, :]
            mixed = total * values[f * QUARTER : (f + 1) * QUARTER, lanes].astype(F32)
            for g in range(f):
                weight = raw[g * QUARTER : (g + 1) * QUARTER, :] * kept[g]
                total += weight
                mixed += weight * values[g * QUARTER : (g + 1) * QUARTER, lanes].astype(F32)
            out_ref[f * QUARTER : (f + 1) * QUARTER, lanes] = (mixed / total).astype(BF16)


def near_kernel(near_rows, mask_ref, weights, near_out, queries, keys, values):
    near_part(near_rows, mask_ref, near_out, weights, queries, keys, values, head_ones())


def far_kernel(keep_ref, far_rows, weights, far_out, queries, keys, values):
    far_part(keep_ref, far_rows, far_out, weights, queries, keys, values, head_ones())


NEAR_SHAPE = jax.ShapeDtypeStruct((OWN_ROWS, HALF), F32)
FAR_SHAPE = jax.ShapeDtypeStruct((FAR_ROWS, HALF), BF16)


def half_call(kernel, shapes, scalars, arrays, key_rows, flops, name):
    whole = pl.BlockSpec(memory_space=pltpu.VMEM)
    return pl.pallas_call(
        kernel,
        out_shape=shapes,
        in_specs=[pl.BlockSpec(memory_space=pltpu.SMEM)] * len(scalars)
        + [whole] * len(arrays),
        out_specs=[whole] * len(shapes),
        scratch_shapes=[
            pltpu.VMEM((OWN_ROWS, HALF), BF16),
            pltpu.VMEM((key_rows, HALF), BF16),
            pltpu.VMEM((key_rows, HALF), BF16),
        ],
        compiler_params=pltpu.CompilerParams(vmem_limit_bytes=VMEM),
        cost_estimate=pl.CostEstimate(flops=flops, bytes_accessed=7 * 10**6, transcendentals=10**6),
        name=name,
    )(*scalars, *arrays)


def out_kernel(
    place_ref, coef_ref, near_a, near_b, f0, f1, f2, f3, weight_a, weight_b, state_ref, noise_ref, out_ref, mixed
):
    frame = place_ref[0]
    core = lax.rem(frame, 2)
    lanes_a = pl.ds(pl.multiple_of(core * HALF, HALF), HALF)
    lanes_b = pl.ds(pl.multiple_of((1 - core) * HALF, HALF), HALF)
    for hop, piece in enumerate((f0, f1, f2, f3)):
        source = lax.rem(frame + 4 - hop, 4)
        for f in range(FRAMES_DEV):
            cells = pl.ds(pl.multiple_of(f * CELLS + source * QUARTER, QUARTER), QUARTER)
            arrived = slice(f * QUARTER, (f + 1) * QUARTER)
            first, second = piece[arrived, :HALF], piece[arrived, HALF:]
            if hop % 2 == 1:
                first, second = second, first
            mixed[cells, lanes_a] = (near_a[cells, :] + first.astype(F32)).astype(BF16)
            mixed[cells, lanes_b] = (near_b[cells, :] + second.astype(F32)).astype(BF16)
    for f in range(FRAMES_DEV):
        rows = slice(f * CELLS, (f + 1) * CELLS)
        for lanes, weight in ((lanes_a, weight_a), (lanes_b, weight_b)):
            update = jnp.dot(mixed[rows, :], weight[...], preferred_element_type=F32)
            out_ref[rows, lanes] = (
                state_ref[rows, lanes].astype(F32)
                + coef_ref[0, f] * update
                + coef_ref[1, f] * noise_ref[rows, lanes].astype(F32)
            ).astype(BF16)


def finish(place_ids, coefs, near_a, near_b, far, weight_a, weight_b, state, noise):
    whole = pl.BlockSpec(memory_space=pltpu.VMEM)
    scalar = pl.BlockSpec(memory_space=pltpu.SMEM)
    return pl.pallas_call(
        out_kernel,
        out_shape=jax.ShapeDtypeStruct((OWN_ROWS, WIDTH), BF16),
        in_specs=[scalar, scalar] + [whole] * 10,
        out_specs=whole,
        scratch_shapes=[pltpu.VMEM((OWN_ROWS, WIDTH), BF16)],
        compiler_params=pltpu.CompilerParams(vmem_limit_bytes=VMEM),
        cost_estimate=pl.CostEstimate(flops=2 * 10**9, bytes_accessed=7 * 10**6, transcendentals=0),
        name="out",
    )(place_ids, coefs, near_a, near_b, *far, weight_a, weight_b, state, noise)


def sigma_of(levels):
    return SIGMA_TOP * jnp.exp(levels.astype(F32) * LOG_DECAY)


def body(latent_state, noise_draws, step_index, keep_frame, qkv_weight, out_weight):
    frame = lax.axis_index("frame")
    lat = lax.axis_index("lat")
    x = lax.axis_index("lon")
    core, z_lo = frame % 2, frame // 2
    z_hi, y = lat // 4, lat % 4

    def arranged(*spots):
        return jnp.stack([jnp.asarray(spot, jnp.int32) % 4 for spot in spots])

    state = latent_state.reshape(OWN_ROWS, WIDTH)
    place_ids = frame.reshape(1).astype(jnp.int32)
    columns = [lax.dynamic_slice(qkv_weight, (0, s * WIDTH + core * HALF), (16, HALF)) for s in range(3)]
    columns.append(lax.dynamic_slice(out_weight, (0, core * HALF), (16, HALF)))
    own_rows = jnp.concatenate(columns, axis=1)
    z_in = [lax.ppermute(own_rows, EVERY, z_routes(slot)) for slot in (1, 2, 3)]
    z_in = [own_rows, *z_in]
    side = 2 * z_lo - 1
    (z_rows,) = place_rows(
        1, arranged(z_hi, z_hi + side, z_hi - side, z_hi + 2), z_in, [(4, 16, 4 * HALF)]
    )
    plane_in = [z_rows] + [lax.ppermute(z_rows, EVERY, plane_routes(2, hop)) for hop in (1, 2, 3)]
    up, down = latent_state[:, ROWS - REACH :], latent_state[:, :REACH]
    up, down, plane_in[1] = lax.optimization_barrier((up, down, plane_in[1]))
    top = lax.ppermute(up, "lat", [(i, i + 1) for i in range(15)])
    bottom = lax.ppermute(down, "lat", [(i + 1, i) for i in range(15)])
    inner, outer = jnp.where(core == 0, y, x), jnp.where(core == 0, x, y)
    plane, plane_out = place_rows(
        2, arranged(inner, inner - 1, inner - 2, inner - 3), plane_in,
        [(4, 4, 16, 3 * HALF), (4, 4, 16, HALF)],
    )
    outer_spots = arranged(outer, outer - 1, outer - 2, outer - 3, core)
    last_in = [plane] + [lax.ppermute(plane, EVERY, plane_routes(3, hop)) for hop in (1, 2, 3)]
    quarters = latent_state.reshape(FRAMES_DEV, 4, QUARTER, WIDTH)

    def quarter(index):
        taken = lax.dynamic_index_in_dim(quarters, index % 4, axis=1, keepdims=False)
        return taken.reshape(FRAMES_DEV * QUARTER, WIDTH)

    sent = [quarter(frame + hop) for hop in (1, 2, 3)]
    *sent, top, bottom = lax.optimization_barrier((*sent, top, bottom))
    far_in = [quarter(frame)] + [lax.ppermute(sent[hop - 1], "frame", frame_routes(hop)) for hop in (1, 2, 3)]
    far_rows = prepare_far(place_ids, far_in)
    *last_in, far_rows, mask, top, bottom = lax.optimization_barrier(
        (*last_in, far_rows, near_mask(lat), top, bottom)
    )
    east, west = edges_of(latent_state, top, bottom)
    *last_in, east, west = lax.optimization_barrier((*last_in, east, west))
    left = lax.ppermute(east, "lon", [(i, (i + 1) % 4) for i in range(4)])
    right = lax.ppermute(west, "lon", [((i + 1) % 4, i) for i in range(4)])
    (weight_a,) = place_rows(3, outer_spots, last_in, [(4, 4, 4, 16, 3 * HALF)])
    weight_a = weight_a.reshape(WIDTH, 3 * HALF)
    weight_b = lax.ppermute(weight_a, EVERY, core_routes())

    (far_a,) = half_call(
        far_kernel, [FAR_SHAPE], [keep_frame], [far_rows, weight_a], FAR_ROWS, 3 * 10**9, "far"
    )
    (far_b,) = half_call(
        far_kernel, [FAR_SHAPE], [keep_frame], [far_rows, weight_b], FAR_ROWS, 3 * 10**9, "far"
    )
    left, right, far_a, far_b = lax.optimization_barrier((left, right, far_a, far_b))
    near_rows = prepare(state, top.reshape(-1, WIDTH), bottom.reshape(-1, WIDTH), left, right)
    plane_out, near_rows = lax.optimization_barrier((plane_out, near_rows))
    far_out = jnp.concatenate([far_a, far_b], axis=1).reshape(4, FRAMES_DEV * QUARTER, WIDTH)

    def frames_of(index):
        return lax.dynamic_index_in_dim(far_out, index % 4, axis=0, keepdims=False)

    far_back = [frames_of(frame)] + [
        lax.ppermute(frames_of(frame + hop), "frame", frame_routes(hop)) for hop in (1, 2, 3)
    ]
    (near_a,) = half_call(
        near_kernel, [NEAR_SHAPE], [], [near_rows, mask, weight_a], NEAR_ROWS, 8 * 10**9, "near"
    )
    out_in = [plane_out] + [lax.ppermute(plane_out, EVERY, plane_routes(3, hop)) for hop in (1, 2, 3)]
    *out_in, near_a = lax.optimization_barrier((*out_in, near_a))
    (out_a,) = place_rows(3, outer_spots, out_in, [(4, 4, 4, 16, HALF)])
    out_a = out_a.reshape(WIDTH, HALF)
    out_b = lax.ppermute(out_a, EVERY, core_routes())
    (near_b,) = half_call(
        near_kernel, [NEAR_SHAPE], [], [near_rows, mask, weight_b], NEAR_ROWS, 8 * 10**9, "near"
    )

    noise_now = sigma_of(step_index)
    noise_next = sigma_of(step_index + 1)
    spread = NOISE_SHARE * jnp.sqrt(noise_now * noise_now - noise_next * noise_next)
    coefs = jnp.stack([noise_next - noise_now, spread])
    denoised = finish(
        place_ids, coefs, near_a, near_b, far_back, out_a, out_b, state, noise_draws.reshape(OWN_ROWS, WIDTH)
    )
    return denoised.reshape(latent_state.shape)


def solution(mesh):
    return jax.shard_map(
        body,
        mesh=mesh,
        in_specs=(
            P("frame", "lat", "lon", None),
            P(None, "frame", "lat", "lon", None),
            P("frame"),
            P(),
            P(("lat", "lon"), None),
            P(("lat", "lon"), None),
        ),
        out_specs=P("frame", "lat", "lon", None),
        check_vma=False,
    )
```

```python
import functools
import math

import jax
import jax.numpy as jnp
from jax import lax
from jax.experimental import pallas as pl
from jax.experimental.pallas import tpu as pltpu
from jax.sharding import PartitionSpec as P

HEAD_DIM = 64
REACH = 6
SIDE = 2 * REACH
SIGMA_TOP = 4.0
LOG_DECAY = math.log(0.8)
NOISE_SHARE = 0.5

FRAMES_DEV = 2
ROWS = 12
COLS = 16
CELLS = ROWS * COLS
WIDTH = 1024
TOTAL_ROWS = 192
FRAMES = 8
QUARTER = CELLS // 4
HALF = WIDTH // 2
QUAD = 256
MID = 176
LOW = MID + ROWS * (COLS + SIDE)
KEYS = LOW + 176
BAND = CELLS // 2
BAND_SKIP = MID
BAND_KEYS = LOW
NEAR_ROWS = FRAMES_DEV * KEYS
FAR_ROWS = FRAMES * QUARTER
OWN_ROWS = FRAMES_DEV * CELLS
VMEM = 32 * 1024 * 1024
BF16 = jnp.bfloat16
F32 = jnp.float32
EVERY = ("frame", "lat", "lon")


def place(z_lo, core, z_hi, y, x):
    return ((z_lo * 2 + core) * 16 + (z_hi % 4) * 4 + y % 4) * 4 + x % 4


def all_places():
    return [
        (z_lo, core, z_hi, y, x)
        for z_lo in range(2)
        for core in range(2)
        for z_hi in range(4)
        for y in range(4)
        for x in range(4)
    ]


def z_routes(slot):
    pairs = []
    for z_lo, core, z_hi, y, x in all_places():
        if slot == 1:
            source = (1 - z_lo, core, z_hi - 1 if z_lo == 0 else z_hi + 1, y, x)
        elif slot == 2:
            source = (z_lo, core, z_hi + 1 if z_lo == 0 else z_hi - 1, y, x)
        else:
            source = (1 - z_lo, core, z_hi + 2, y, x)
        pairs.append((place(*source), place(z_lo, core, z_hi, y, x)))
    return pairs


def plane_routes(stage, hop):
    pairs = []
    for z_lo, core, z_hi, y, x in all_places():
        along_y = (core == 0) == (stage == 2)
        target = (z_lo, core, z_hi, y + hop, x) if along_y else (z_lo, core, z_hi, y, x + hop)
        pairs.append((place(z_lo, core, z_hi, y, x), place(*target)))
    return pairs


def core_routes():
    return [(place(zl, c, zh, y, x), place(zl, 1 - c, zh, y, x)) for zl, c, zh, y, x in all_places()]


def frame_routes(hop):
    return [(p, (p + hop) % 4) for p in range(4)]


def place_kernel(mode, spots_ref, *refs):
    arrived, targets = refs[:4], refs[4:]
    split = 3 * HALF

    def run(by_first):
        for d in range(4):
            spot = spots_ref[d]
            if mode == 1:
                targets[0][spot] = arrived[d][...]
                continue

            def step(z, carry, d=d, spot=spot):
                if mode == 2:
                    targets[0][z, spot] = arrived[d][z, :, :split]
                    targets[1][z, spot] = arrived[d][z, :, split:]
                elif by_first:
                    targets[0][z, spot] = arrived[d][z]
                else:
                    targets[0][z, :, spot] = arrived[d][z]
                return carry

            lax.fori_loop(0, 4, step, 0)

    if mode < 3:
        run(False)
    else:
        pl.when(spots_ref[4] == 0)(lambda: run(False))
        pl.when(spots_ref[4] == 1)(lambda: run(True))


def place_rows(mode, spots, arrived, shapes):
    whole = pl.BlockSpec(memory_space=pltpu.VMEM)
    size = sum(2 * math.prod(shape) for shape in shapes)
    return pl.pallas_call(
        functools.partial(place_kernel, mode),
        out_shape=[jax.ShapeDtypeStruct(shape, BF16) for shape in shapes],
        in_specs=[pl.BlockSpec(memory_space=pltpu.SMEM)] + [whole] * 4,
        out_specs=[whole] * len(shapes),
        compiler_params=pltpu.CompilerParams(vmem_limit_bytes=VMEM),
        cost_estimate=pl.CostEstimate(flops=0, bytes_accessed=2 * size, transcendentals=0),
        name="place",
    )(spots, *arrived)


def near_mask(lat):
    spot = jnp.arange(BAND_KEYS, dtype=jnp.int32)[None, :]
    cell = jnp.arange(CELLS, dtype=jnp.int32)[:, None]
    spot = spot + jnp.where(cell < CELLS // 2, 0, BAND_SKIP)
    part = jnp.where(spot < MID, 0, jnp.where(spot < LOW, 1, 2))
    base = jnp.where(part == 0, 0, jnp.where(part == 1, MID, LOW))
    first_row = jnp.where(part == 0, 0, jnp.where(part == 1, REACH, REACH + ROWS))
    tall = jnp.where(part == 1, ROWS, REACH)
    local = spot - base
    centre = tall * COLS
    edge = tall * REACH
    side = local - centre
    right = side >= edge
    side = jnp.where(right, side - edge, side)
    inner = local < centre
    key_row = first_row + jnp.where(inner, local // COLS, side // REACH)
    key_col = jnp.where(
        inner, REACH + local % COLS, jnp.where(right, COLS + REACH, 0) + side % REACH
    )
    lat_gap = key_row - cell // COLS
    lon_gap = key_col - cell % COLS
    global_row = lat * ROWS + key_row - REACH
    inside = (global_row >= 0) & (global_row < TOTAL_ROWS) & (local < centre + 2 * edge)
    seen = (lat_gap >= 0) & (lat_gap <= SIDE) & (lon_gap >= 0) & (lon_gap <= SIDE)
    return (seen & inside).astype(BF16)


def edge_kernel(own, top, bottom, east, west, east_tmp, west_tmp):
    for f in range(FRAMES_DEV):
        for row in range(ROWS + SIDE):
            if row < REACH:
                block = top[f, row]
            elif row < REACH + ROWS:
                block = own[f, row - REACH]
            else:
                block = bottom[f, row - REACH - ROWS]
            block = block.astype(F32)
            start = (f * (ROWS + SIDE) + row) * REACH
            east_tmp[start : start + REACH, :] = block[COLS - REACH :]
            west_tmp[start : start + REACH, :] = block[:REACH]
    east[...] = east_tmp[...].astype(BF16)
    west[...] = west_tmp[...].astype(BF16)


def edges_of(own, top, bottom):
    whole = pl.BlockSpec(memory_space=pltpu.VMEM)
    rows = FRAMES_DEV * (ROWS + SIDE) * REACH
    return pl.pallas_call(
        edge_kernel,
        out_shape=[jax.ShapeDtypeStruct((rows, WIDTH), BF16)] * 2,
        in_specs=[whole] * 3,
        out_specs=[whole] * 2,
        scratch_shapes=[pltpu.VMEM((rows, WIDTH), F32)] * 2,
        compiler_params=pltpu.CompilerParams(vmem_limit_bytes=VMEM),
        cost_estimate=pl.CostEstimate(flops=10**6, bytes_accessed=3 * 10**6, transcendentals=0),
        name="edges",
    )(own, top, bottom)


def normed(block):
    rows = block.astype(F32)
    return rows * lax.rsqrt(jnp.mean(rows * rows, axis=-1, keepdims=True) + 1e-05)


def prep_kernel(own, top, bottom, left, right, near_out, rows_tmp, edge_tmp):
    def place_rows(source, start, offset, count):
        def step(index, carry):
            taken = source[pl.ds(pl.multiple_of(start + index * 48, 16), 48), :]
            rows_tmp[pl.ds(pl.multiple_of(offset + index * 48, 16), 48), :] = normed(taken)
            return carry

        lax.fori_loop(0, count // 48, step, 0)

    for f in range(FRAMES_DEV):
        base = f * KEYS
        place_rows(own, f * CELLS, base + MID, CELLS)
        place_rows(top, f * 96, base, 96)
        place_rows(bottom, f * 96, base + LOW, 96)
        rows_tmp[base + MID - 8 : base + MID, :] = jnp.zeros((8, WIDTH), F32)
        rows_tmp[base + KEYS - 8 : base + KEYS, :] = jnp.zeros((8, WIDTH), F32)
    for index, edge in enumerate((left, right)):
        for chunk in range(6):
            spot = slice(chunk * 48, (chunk + 1) * 48)
            edge_tmp[spot, :] = normed(edge[spot, :])
        for f in range(FRAMES_DEV):
            for first, count, target in (
                (0, 36, 96 + index * 36),
                (36, 72, MID + CELLS + index * 72),
                (108, 36, LOW + 96 + index * 36),
            ):
                start = f * 144 + first
                rows_tmp[f * KEYS + target : f * KEYS + target + count, :] = edge_tmp[start : start + count, :]

    def settle(index, carry):
        rows = pl.ds(pl.multiple_of(index * 32, 32), 32)
        near_out[rows, :] = rows_tmp[rows, :].astype(BF16)
        return carry

    lax.fori_loop(0, NEAR_ROWS // 32, settle, 0)

def far_prep_kernel(frame_ref, f0, f1, f2, f3, far_out):
    for hop, piece in enumerate((f0, f1, f2, f3)):
        source = lax.rem(frame_ref[0] + 4 - hop, 4)

        def far_step(index, carry, piece=piece, source=source):
            taken = piece[pl.ds(pl.multiple_of(index * 48, 16), 48), :]
            target = pl.ds(pl.multiple_of(source * (2 * QUARTER) + index * 48, 16), 48)
            far_out[target, :] = normed(taken).astype(BF16)
            return carry

        lax.fori_loop(0, 2, far_step, 0)


def prepare_far(frame, far):
    whole = pl.BlockSpec(memory_space=pltpu.VMEM)
    return pl.pallas_call(
        far_prep_kernel,
        out_shape=jax.ShapeDtypeStruct((FAR_ROWS, WIDTH), BF16),
        in_specs=[pl.BlockSpec(memory_space=pltpu.SMEM)] + [whole] * 4,
        out_specs=whole,
        compiler_params=pltpu.CompilerParams(vmem_limit_bytes=VMEM),
        cost_estimate=pl.CostEstimate(flops=10**8, bytes_accessed=16 * 10**5, transcendentals=0),
        name="prep_far",
    )(frame, *far)


def prepare(own, top, bottom, left, right):
    whole = pl.BlockSpec(memory_space=pltpu.VMEM)
    return pl.pallas_call(
        prep_kernel,
        out_shape=jax.ShapeDtypeStruct((NEAR_ROWS, WIDTH), BF16),
        in_specs=[whole] * 5,
        out_specs=whole,
        scratch_shapes=[pltpu.VMEM((NEAR_ROWS, WIDTH), F32), pltpu.VMEM((288, WIDTH), F32)],
        compiler_params=pltpu.CompilerParams(vmem_limit_bytes=VMEM),
        cost_estimate=pl.CostEstimate(flops=10**9, bytes_accessed=8 * 10**6, transcendentals=0),
        name="prep",
    )(own, top, bottom, left, right)


def head_ones():
    row = lax.broadcasted_iota(jnp.int32, (QUAD, QUAD), 0) // HEAD_DIM
    col = lax.broadcasted_iota(jnp.int32, (QUAD, QUAD), 1) // HEAD_DIM
    return jnp.where(row == col, 1.0, 0.0).astype(BF16)


def head_scale(values, ones):
    squares = jnp.dot((values * values).astype(BF16), ones, preferred_element_type=F32)
    return values * lax.rsqrt(squares * (1.0 / HEAD_DIM) + 1e-06)


def scaled_heads(rows, weights, part, ones, target, spot, factor):
    found = jnp.dot(rows, weights[:, part * HALF : (part + 1) * HALF], preferred_element_type=F32)
    for quad in range(2):
        lanes = slice(quad * QUAD, (quad + 1) * QUAD)
        target[spot, lanes] = head_scale(found[:, lanes], ones).astype(BF16) * jnp.bfloat16(factor)


def near_part(rows_ref, mask_ref, out_ref, weights, queries, keys, values, ones):
    def key_step(index, carry):
        spot = pl.ds(pl.multiple_of(index * KEYS, 16), KEYS)
        block = rows_ref[spot, :]
        scaled_heads(block, weights, 1, ones, keys, spot, 1.0)
        values[spot, :] = jnp.dot(block, weights[:, 2 * HALF :], preferred_element_type=F32).astype(BF16)
        cells = rows_ref[pl.ds(pl.multiple_of(index * KEYS + MID, 16), CELLS), :]
        target = pl.ds(pl.multiple_of(index * CELLS, CELLS), CELLS)
        scaled_heads(cells, weights, 0, ones, queries, target, HEAD_DIM**-0.5)
        return carry

    lax.fori_loop(0, FRAMES_DEV, key_step, 0)

    head = lax.broadcasted_iota(jnp.int32, (BAND, QUAD), 1) // HEAD_DIM

    def attend(f, quad, band):
        lanes = slice(quad * QUAD, (quad + 1) * QUAD)
        cells = pl.ds(pl.multiple_of(f * CELLS + band * BAND, BAND), BAND)
        spots = pl.ds(pl.multiple_of(f * KEYS + band * BAND_SKIP, 16), BAND_KEYS)
        query = queries[cells, lanes]
        stacked = jnp.concatenate(
            [jnp.where(head == member, query, jnp.bfloat16(0.0)) for member in range(4)], axis=0
        )
        scores = lax.dot_general(
            stacked, keys[spots, lanes], (((1,), (1,)), ((), ())), preferred_element_type=F32
        )
        seen = mask_ref[band * BAND : (band + 1) * BAND, :]
        raw = jnp.exp(scores).astype(BF16) * jnp.concatenate([seen] * 4, axis=0)
        found = jnp.dot(raw, values[spots, lanes], preferred_element_type=F32)
        found = found / jnp.sum(raw.astype(F32), axis=-1, keepdims=True)
        result = found[:BAND]
        for member in range(1, 4):
            result = jnp.where(head == member, found[member * BAND : (member + 1) * BAND], result)
        out_ref[cells, lanes] = result

    def step(f, carry):
        for quad in range(2):
            for band in range(2):
                attend(f, quad, band)
        return carry

    lax.fori_loop(0, FRAMES_DEV, step, 0)


def far_part(keep_ref, rows_ref, out_ref, weights, queries, keys, values, ones):
    block, every = rows_ref[...], slice(0, FAR_ROWS)
    scaled_heads(block, weights, 0, ones, queries, every, HEAD_DIM**-0.5)
    scaled_heads(block, weights, 1, ones, keys, every, 1.0)
    values[every, :] = jnp.dot(block, weights[:, 2 * HALF :], preferred_element_type=F32).astype(BF16)
    kept = [jnp.where(keep_ref[g] == 1, 1.0, 0.0).astype(F32) for g in range(FRAMES)]
    for quad in range(2):
        lanes = slice(quad * QUAD, (quad + 1) * QUAD)
        for f in range(FRAMES):
            query = queries[f * QUARTER : (f + 1) * QUARTER, lanes]
            products = [query * keys[g * QUARTER : (g + 1) * QUARTER, lanes] for g in range(f + 1)]
            scores = jnp.dot(jnp.concatenate(products, axis=0), ones, preferred_element_type=F32)
            raw = jnp.exp(scores)
            total = raw[f * QUARTER :, :]
            mixed = total * values[f * QUARTER : (f + 1) * QUARTER, lanes].astype(F32)
            for g in range(f):
                weight = raw[g * QUARTER : (g + 1) * QUARTER, :] * kept[g]
                total += weight
                mixed += weight * values[g * QUARTER : (g + 1) * QUARTER, lanes].astype(F32)
            out_ref[f * QUARTER : (f + 1) * QUARTER, lanes] = (mixed / total).astype(BF16)


def near_kernel(near_rows, mask_ref, weights, near_out, queries, keys, values):
    near_part(near_rows, mask_ref, near_out, weights, queries, keys, values, head_ones())


def far_kernel(keep_ref, far_rows, weights, far_out, queries, keys, values):
    far_part(keep_ref, far_rows, far_out, weights, queries, keys, values, head_ones())


NEAR_SHAPE = jax.ShapeDtypeStruct((OWN_ROWS, HALF), F32)
FAR_SHAPE = jax.ShapeDtypeStruct((FAR_ROWS, HALF), BF16)


def half_call(kernel, shapes, scalars, arrays, key_rows, flops, name):
    whole = pl.BlockSpec(memory_space=pltpu.VMEM)
    return pl.pallas_call(
        kernel,
        out_shape=shapes,
        in_specs=[pl.BlockSpec(memory_space=pltpu.SMEM)] * len(scalars)
        + [whole] * len(arrays),
        out_specs=[whole] * len(shapes),
        scratch_shapes=[
            pltpu.VMEM((OWN_ROWS, HALF), BF16),
            pltpu.VMEM((key_rows, HALF), BF16),
            pltpu.VMEM((key_rows, HALF), BF16),
        ],
        compiler_params=pltpu.CompilerParams(vmem_limit_bytes=VMEM),
        cost_estimate=pl.CostEstimate(flops=flops, bytes_accessed=7 * 10**6, transcendentals=10**6),
        name=name,
    )(*scalars, *arrays)


def out_kernel(
    place_ref, coef_ref, near_a, near_b, f0, f1, f2, f3, weight_a, weight_b, state_ref, noise_ref, out_ref, mixed
):
    frame = place_ref[0]
    core = lax.rem(frame, 2)
    lanes_a = pl.ds(pl.multiple_of(core * HALF, HALF), HALF)
    lanes_b = pl.ds(pl.multiple_of((1 - core) * HALF, HALF), HALF)
    for hop, piece in enumerate((f0, f1, f2, f3)):
        source = lax.rem(frame + 4 - hop, 4)
        for f in range(FRAMES_DEV):
            cells = pl.ds(pl.multiple_of(f * CELLS + source * QUARTER, QUARTER), QUARTER)
            arrived = slice(f * QUARTER, (f + 1) * QUARTER)
            first, second = piece[arrived, :HALF], piece[arrived, HALF:]
            if hop % 2 == 1:
                first, second = second, first
            mixed[cells, lanes_a] = (near_a[cells, :] + first.astype(F32)).astype(BF16)
            mixed[cells, lanes_b] = (near_b[cells, :] + second.astype(F32)).astype(BF16)
    for f in range(FRAMES_DEV):
        rows = slice(f * CELLS, (f + 1) * CELLS)
        for lanes, weight in ((lanes_a, weight_a), (lanes_b, weight_b)):
            update = jnp.dot(mixed[rows, :], weight[...], preferred_element_type=F32)
            out_ref[rows, lanes] = (
                state_ref[rows, lanes].astype(F32)
                + coef_ref[0, f] * update
                + coef_ref[1, f] * noise_ref[rows, lanes].astype(F32)
            ).astype(BF16)


def finish(place_ids, coefs, near_a, near_b, far, weight_a, weight_b, state, noise):
    whole = pl.BlockSpec(memory_space=pltpu.VMEM)
    scalar = pl.BlockSpec(memory_space=pltpu.SMEM)
    return pl.pallas_call(
        out_kernel,
        out_shape=jax.ShapeDtypeStruct((OWN_ROWS, WIDTH), BF16),
        in_specs=[scalar, scalar] + [whole] * 10,
        out_specs=whole,
        scratch_shapes=[pltpu.VMEM((OWN_ROWS, WIDTH), BF16)],
        compiler_params=pltpu.CompilerParams(vmem_limit_bytes=VMEM),
        cost_estimate=pl.CostEstimate(flops=2 * 10**9, bytes_accessed=7 * 10**6, transcendentals=0),
        name="out",
    )(place_ids, coefs, near_a, near_b, *far, weight_a, weight_b, state, noise)


def sigma_of(levels):
    return SIGMA_TOP * jnp.exp(levels.astype(F32) * LOG_DECAY)


def body(latent_state, noise_draws, step_index, keep_frame, qkv_weight, out_weight):
    frame = lax.axis_index("frame")
    lat = lax.axis_index("lat")
    x = lax.axis_index("lon")
    core, z_lo = frame % 2, frame // 2
    z_hi, y = lat // 4, lat % 4

    def arranged(*spots):
        return jnp.stack([jnp.asarray(spot, jnp.int32) % 4 for spot in spots])

    state = latent_state.reshape(OWN_ROWS, WIDTH)
    place_ids = frame.reshape(1).astype(jnp.int32)
    columns = [lax.dynamic_slice(qkv_weight, (0, s * WIDTH + core * HALF), (16, HALF)) for s in range(3)]
    columns.append(lax.dynamic_slice(out_weight, (0, core * HALF), (16, HALF)))
    own_rows = jnp.concatenate(columns, axis=1)
    z_in = [lax.ppermute(own_rows, EVERY, z_routes(slot)) for slot in (1, 2, 3)]
    z_in = [own_rows, *z_in]
    side = 2 * z_lo - 1
    (z_rows,) = place_rows(
        1, arranged(z_hi, z_hi + side, z_hi - side, z_hi + 2), z_in, [(4, 16, 4 * HALF)]
    )
    plane_in = [z_rows] + [lax.ppermute(z_rows, EVERY, plane_routes(2, hop)) for hop in (1, 2, 3)]
    up, down = latent_state[:, ROWS - REACH :], latent_state[:, :REACH]
    up, down, plane_in[1] = lax.optimization_barrier((up, down, plane_in[1]))
    top = lax.ppermute(up, "lat", [(i, i + 1) for i in range(15)])
    bottom = lax.ppermute(down, "lat", [(i + 1, i) for i in range(15)])
    inner, outer = jnp.where(core == 0, y, x), jnp.where(core == 0, x, y)
    plane, plane_out = place_rows(
        2, arranged(inner, inner - 1, inner - 2, inner - 3), plane_in,
        [(4, 4, 16, 3 * HALF), (4, 4, 16, HALF)],
    )
    outer_spots = arranged(outer, outer - 1, outer - 2, outer - 3, core)
    last_in = [plane] + [lax.ppermute(plane, EVERY, plane_routes(3, hop)) for hop in (1, 2, 3)]
    quarters = latent_state.reshape(FRAMES_DEV, 4, QUARTER, WIDTH)

    def quarter(index):
        taken = lax.dynamic_index_in_dim(quarters, index % 4, axis=1, keepdims=False)
        return taken.reshape(FRAMES_DEV * QUARTER, WIDTH)

    sent = [quarter(frame + hop) for hop in (1, 2, 3)]
    *sent, top, bottom = lax.optimization_barrier((*sent, top, bottom))
    far_in = [quarter(frame)] + [lax.ppermute(sent[hop - 1], "frame", frame_routes(hop)) for hop in (1, 2, 3)]
    far_rows = prepare_far(place_ids, far_in)
    *last_in, far_rows, mask, top, bottom = lax.optimization_barrier(
        (*last_in, far_rows, near_mask(lat), top, bottom)
    )
    east, west = edges_of(latent_state, top, bottom)
    *last_in, east, west = lax.optimization_barrier((*last_in, east, west))
    left = lax.ppermute(east, "lon", [(i, (i + 1) % 4) for i in range(4)])
    right = lax.ppermute(west, "lon", [((i + 1) % 4, i) for i in range(4)])
    (weight_a,) = place_rows(3, outer_spots, last_in, [(4, 4, 4, 16, 3 * HALF)])
    weight_a = weight_a.reshape(WIDTH, 3 * HALF)
    weight_b = lax.ppermute(weight_a, EVERY, core_routes())

    (far_a,) = half_call(
        far_kernel, [FAR_SHAPE], [keep_frame], [far_rows, weight_a], FAR_ROWS, 3 * 10**9, "far"
    )
    (far_b,) = half_call(
        far_kernel, [FAR_SHAPE], [keep_frame], [far_rows, weight_b], FAR_ROWS, 3 * 10**9, "far"
    )
    left, right, far_a, far_b = lax.optimization_barrier((left, right, far_a, far_b))
    near_rows = prepare(state, top.reshape(-1, WIDTH), bottom.reshape(-1, WIDTH), left, right)
    plane_out, near_rows = lax.optimization_barrier((plane_out, near_rows))
    far_out = jnp.concatenate([far_a, far_b], axis=1).reshape(4, FRAMES_DEV * QUARTER, WIDTH)

    def frames_of(index):
        return lax.dynamic_index_in_dim(far_out, index % 4, axis=0, keepdims=False)

    far_back = [frames_of(frame)] + [
        lax.ppermute(frames_of(frame + hop), "frame", frame_routes(hop)) for hop in (1, 2, 3)
    ]
    (near_a,) = half_call(
        near_kernel, [NEAR_SHAPE], [], [near_rows, mask, weight_a], NEAR_ROWS, 8 * 10**9, "near"
    )
    out_in = [plane_out] + [lax.ppermute(plane_out, EVERY, plane_routes(3, hop)) for hop in (1, 2, 3)]
    *out_in, near_a, far_back[1], far_back[2] = lax.optimization_barrier(
        (*out_in, near_a, far_back[1], far_back[2])
    )
    (out_a,) = place_rows(3, outer_spots, out_in, [(4, 4, 4, 16, HALF)])
    out_a = out_a.reshape(WIDTH, HALF)
    out_b = lax.ppermute(out_a, EVERY, core_routes())
    (near_b,) = half_call(
        near_kernel, [NEAR_SHAPE], [], [near_rows, mask, weight_b], NEAR_ROWS, 8 * 10**9, "near"
    )

    noise_now = sigma_of(step_index)
    noise_next = sigma_of(step_index + 1)
    spread = NOISE_SHARE * jnp.sqrt(noise_now * noise_now - noise_next * noise_next)
    coefs = jnp.stack([noise_next - noise_now, spread])
    denoised = finish(
        place_ids, coefs, near_a, near_b, far_back, out_a, out_b, state, noise_draws.reshape(OWN_ROWS, WIDTH)
    )
    return denoised.reshape(latent_state.shape)


def solution(mesh):
    return jax.shard_map(
        body,
        mesh=mesh,
        in_specs=(
            P("frame", "lat", "lon", None),
            P(None, "frame", "lat", "lon", None),
            P("frame"),
            P(),
            P(("lat", "lon"), None),
            P(("lat", "lon"), None),
        ),
        out_specs=P("frame", "lat", "lon", None),
        check_vma=False,
    )
```

```python
import functools
import math

import jax
import jax.numpy as jnp
from jax import lax
from jax.experimental import pallas as pl
from jax.experimental.pallas import tpu as pltpu
from jax.sharding import PartitionSpec as P

HEAD_DIM = 64
REACH = 6
SIDE = 2 * REACH
SIGMA_TOP = 4.0
LOG_DECAY = math.log(0.8)
NOISE_SHARE = 0.5

FRAMES_DEV = 2
ROWS = 12
COLS = 16
CELLS = ROWS * COLS
WIDTH = 1024
TOTAL_ROWS = 192
FRAMES = 8
QUARTER = CELLS // 4
HALF = WIDTH // 2
QUAD = 256
MID = 176
LOW = MID + ROWS * (COLS + SIDE)
KEYS = LOW + 176
BAND = CELLS // 2
BAND_SKIP = MID
BAND_KEYS = LOW
NEAR_ROWS = FRAMES_DEV * KEYS
FAR_ROWS = FRAMES * QUARTER
OWN_ROWS = FRAMES_DEV * CELLS
VMEM = 32 * 1024 * 1024
BF16 = jnp.bfloat16
F32 = jnp.float32
EVERY = ("frame", "lat", "lon")


def place(z_lo, core, z_hi, y, x):
    return ((z_lo * 2 + core) * 16 + (z_hi % 4) * 4 + y % 4) * 4 + x % 4


def all_places():
    return [
        (z_lo, core, z_hi, y, x)
        for z_lo in range(2)
        for core in range(2)
        for z_hi in range(4)
        for y in range(4)
        for x in range(4)
    ]


def z_routes(slot):
    pairs = []
    for z_lo, core, z_hi, y, x in all_places():
        if slot == 1:
            source = (1 - z_lo, core, z_hi - 1 if z_lo == 0 else z_hi + 1, y, x)
        elif slot == 2:
            source = (z_lo, core, z_hi + 1 if z_lo == 0 else z_hi - 1, y, x)
        else:
            source = (1 - z_lo, core, z_hi + 2, y, x)
        pairs.append((place(*source), place(z_lo, core, z_hi, y, x)))
    return pairs


def plane_routes(stage, hop):
    pairs = []
    for z_lo, core, z_hi, y, x in all_places():
        along_y = (core == 0) == (stage == 2)
        target = (z_lo, core, z_hi, y + hop, x) if along_y else (z_lo, core, z_hi, y, x + hop)
        pairs.append((place(z_lo, core, z_hi, y, x), place(*target)))
    return pairs


def core_routes():
    return [(place(zl, c, zh, y, x), place(zl, 1 - c, zh, y, x)) for zl, c, zh, y, x in all_places()]


def frame_routes(hop):
    return [(p, (p + hop) % 4) for p in range(4)]


def place_kernel(mode, spots_ref, *refs):
    arrived, targets = refs[:4], refs[4:]
    split = 3 * HALF

    def run(by_first):
        for d in range(4):
            spot = spots_ref[d]
            if mode == 1:
                targets[0][spot] = arrived[d][...]
                continue

            def step(z, carry, d=d, spot=spot):
                if mode == 2:
                    targets[0][z, spot] = arrived[d][z, :, :split]
                    targets[1][z, spot] = arrived[d][z, :, split:]
                elif by_first:
                    targets[0][z, spot] = arrived[d][z]
                else:
                    targets[0][z, :, spot] = arrived[d][z]
                return carry

            lax.fori_loop(0, 4, step, 0)

    if mode < 3:
        run(False)
    else:
        pl.when(spots_ref[4] == 0)(lambda: run(False))
        pl.when(spots_ref[4] == 1)(lambda: run(True))


def place_rows(mode, spots, arrived, shapes):
    whole = pl.BlockSpec(memory_space=pltpu.VMEM)
    size = sum(2 * math.prod(shape) for shape in shapes)
    return pl.pallas_call(
        functools.partial(place_kernel, mode),
        out_shape=[jax.ShapeDtypeStruct(shape, BF16) for shape in shapes],
        in_specs=[pl.BlockSpec(memory_space=pltpu.SMEM)] + [whole] * 4,
        out_specs=[whole] * len(shapes),
        compiler_params=pltpu.CompilerParams(vmem_limit_bytes=VMEM),
        cost_estimate=pl.CostEstimate(flops=0, bytes_accessed=2 * size, transcendentals=0),
        name="place",
    )(spots, *arrived)


def near_mask(lat):
    spot = jnp.arange(BAND_KEYS, dtype=jnp.int32)[None, :]
    cell = jnp.arange(CELLS, dtype=jnp.int32)[:, None]
    spot = spot + jnp.where(cell < CELLS // 2, 0, BAND_SKIP)
    part = jnp.where(spot < MID, 0, jnp.where(spot < LOW, 1, 2))
    base = jnp.where(part == 0, 0, jnp.where(part == 1, MID, LOW))
    first_row = jnp.where(part == 0, 0, jnp.where(part == 1, REACH, REACH + ROWS))
    tall = jnp.where(part == 1, ROWS, REACH)
    local = spot - base
    centre = tall * COLS
    edge = tall * REACH
    side = local - centre
    right = side >= edge
    side = jnp.where(right, side - edge, side)
    inner = local < centre
    key_row = first_row + jnp.where(inner, local // COLS, side // REACH)
    key_col = jnp.where(
        inner, REACH + local % COLS, jnp.where(right, COLS + REACH, 0) + side % REACH
    )
    lat_gap = key_row - cell // COLS
    lon_gap = key_col - cell % COLS
    global_row = lat * ROWS + key_row - REACH
    inside = (global_row >= 0) & (global_row < TOTAL_ROWS) & (local < centre + 2 * edge)
    seen = (lat_gap >= 0) & (lat_gap <= SIDE) & (lon_gap >= 0) & (lon_gap <= SIDE)
    return (seen & inside).astype(BF16)


def edge_kernel(own, top, bottom, east, west, east_tmp, west_tmp):
    for f in range(FRAMES_DEV):
        for row in range(ROWS + SIDE):
            if row < REACH:
                block = top[f, row]
            elif row < REACH + ROWS:
                block = own[f, row - REACH]
            else:
                block = bottom[f, row - REACH - ROWS]
            block = block.astype(F32)
            start = (f * (ROWS + SIDE) + row) * REACH
            east_tmp[start : start + REACH, :] = block[COLS - REACH :]
            west_tmp[start : start + REACH, :] = block[:REACH]
    east[...] = east_tmp[...].astype(BF16)
    west[...] = west_tmp[...].astype(BF16)


def edges_of(own, top, bottom):
    whole = pl.BlockSpec(memory_space=pltpu.VMEM)
    rows = FRAMES_DEV * (ROWS + SIDE) * REACH
    return pl.pallas_call(
        edge_kernel,
        out_shape=[jax.ShapeDtypeStruct((rows, WIDTH), BF16)] * 2,
        in_specs=[whole] * 3,
        out_specs=[whole] * 2,
        scratch_shapes=[pltpu.VMEM((rows, WIDTH), F32)] * 2,
        compiler_params=pltpu.CompilerParams(vmem_limit_bytes=VMEM),
        cost_estimate=pl.CostEstimate(flops=10**6, bytes_accessed=3 * 10**6, transcendentals=0),
        name="edges",
    )(own, top, bottom)


def normed(block):
    rows = block.astype(F32)
    return rows * lax.rsqrt(jnp.mean(rows * rows, axis=-1, keepdims=True) + 1e-05)


def prep_kernel(own, top, bottom, left, right, near_out, rows_tmp, edge_tmp):
    def place_rows(source, start, offset, count):
        def step(index, carry):
            taken = source[pl.ds(pl.multiple_of(start + index * 48, 16), 48), :]
            rows_tmp[pl.ds(pl.multiple_of(offset + index * 48, 16), 48), :] = normed(taken)
            return carry

        lax.fori_loop(0, count // 48, step, 0)

    for f in range(FRAMES_DEV):
        base = f * KEYS
        place_rows(own, f * CELLS, base + MID, CELLS)
        place_rows(top, f * 96, base, 96)
        place_rows(bottom, f * 96, base + LOW, 96)
        rows_tmp[base + MID - 8 : base + MID, :] = jnp.zeros((8, WIDTH), F32)
        rows_tmp[base + KEYS - 8 : base + KEYS, :] = jnp.zeros((8, WIDTH), F32)
    for index, edge in enumerate((left, right)):
        for chunk in range(6):
            spot = slice(chunk * 48, (chunk + 1) * 48)
            edge_tmp[spot, :] = normed(edge[spot, :])
        for f in range(FRAMES_DEV):
            for first, count, target in (
                (0, 36, 96 + index * 36),
                (36, 72, MID + CELLS + index * 72),
                (108, 36, LOW + 96 + index * 36),
            ):
                start = f * 144 + first
                rows_tmp[f * KEYS + target : f * KEYS + target + count, :] = edge_tmp[start : start + count, :]

    def settle(index, carry):
        rows = pl.ds(pl.multiple_of(index * 32, 32), 32)
        near_out[rows, :] = rows_tmp[rows, :].astype(BF16)
        return carry

    lax.fori_loop(0, NEAR_ROWS // 32, settle, 0)

def far_prep_kernel(frame_ref, f0, f1, f2, f3, far_out):
    for hop, piece in enumerate((f0, f1, f2, f3)):
        source = lax.rem(frame_ref[0] + 4 - hop, 4)

        def far_step(index, carry, piece=piece, source=source):
            taken = piece[pl.ds(pl.multiple_of(index * 48, 16), 48), :]
            target = pl.ds(pl.multiple_of(source * (2 * QUARTER) + index * 48, 16), 48)
            far_out[target, :] = normed(taken).astype(BF16)
            return carry

        lax.fori_loop(0, 2, far_step, 0)


def prepare_far(frame, far):
    whole = pl.BlockSpec(memory_space=pltpu.VMEM)
    return pl.pallas_call(
        far_prep_kernel,
        out_shape=jax.ShapeDtypeStruct((FAR_ROWS, WIDTH), BF16),
        in_specs=[pl.BlockSpec(memory_space=pltpu.SMEM)] + [whole] * 4,
        out_specs=whole,
        compiler_params=pltpu.CompilerParams(vmem_limit_bytes=VMEM),
        cost_estimate=pl.CostEstimate(flops=10**8, bytes_accessed=16 * 10**5, transcendentals=0),
        name="prep_far",
    )(frame, *far)


def prepare(own, top, bottom, left, right):
    whole = pl.BlockSpec(memory_space=pltpu.VMEM)
    return pl.pallas_call(
        prep_kernel,
        out_shape=jax.ShapeDtypeStruct((NEAR_ROWS, WIDTH), BF16),
        in_specs=[whole] * 5,
        out_specs=whole,
        scratch_shapes=[pltpu.VMEM((NEAR_ROWS, WIDTH), F32), pltpu.VMEM((288, WIDTH), F32)],
        compiler_params=pltpu.CompilerParams(vmem_limit_bytes=VMEM),
        cost_estimate=pl.CostEstimate(flops=10**9, bytes_accessed=8 * 10**6, transcendentals=0),
        name="prep",
    )(own, top, bottom, left, right)


def head_ones():
    row = lax.broadcasted_iota(jnp.int32, (QUAD, QUAD), 0) // HEAD_DIM
    col = lax.broadcasted_iota(jnp.int32, (QUAD, QUAD), 1) // HEAD_DIM
    return jnp.where(row == col, 1.0, 0.0).astype(BF16)


def head_scale(values, ones):
    squares = jnp.dot((values * values).astype(BF16), ones, preferred_element_type=F32)
    return values * lax.rsqrt(squares * (1.0 / HEAD_DIM) + 1e-06)


def scaled_heads(rows, weights, part, ones, target, spot, factor):
    found = jnp.dot(rows, weights[:, part * HALF : (part + 1) * HALF], preferred_element_type=F32)
    for quad in range(2):
        lanes = slice(quad * QUAD, (quad + 1) * QUAD)
        target[spot, lanes] = head_scale(found[:, lanes], ones).astype(BF16) * jnp.bfloat16(factor)


def near_part(rows_ref, mask_ref, out_ref, weights, queries, keys, values, ones):
    def key_step(index, carry):
        spot = pl.ds(pl.multiple_of(index * KEYS, 16), KEYS)
        block = rows_ref[spot, :]
        scaled_heads(block, weights, 1, ones, keys, spot, 1.0)
        values[spot, :] = jnp.dot(block, weights[:, 2 * HALF :], preferred_element_type=F32).astype(BF16)
        cells = rows_ref[pl.ds(pl.multiple_of(index * KEYS + MID, 16), CELLS), :]
        target = pl.ds(pl.multiple_of(index * CELLS, CELLS), CELLS)
        scaled_heads(cells, weights, 0, ones, queries, target, HEAD_DIM**-0.5)
        return carry

    lax.fori_loop(0, FRAMES_DEV, key_step, 0)

    head = lax.broadcasted_iota(jnp.int32, (BAND, QUAD), 1) // HEAD_DIM

    def attend(f, quad, band):
        lanes = slice(quad * QUAD, (quad + 1) * QUAD)
        cells = pl.ds(pl.multiple_of(f * CELLS + band * BAND, BAND), BAND)
        spots = pl.ds(pl.multiple_of(f * KEYS + band * BAND_SKIP, 16), BAND_KEYS)
        query = queries[cells, lanes]
        stacked = jnp.concatenate(
            [jnp.where(head == member, query, jnp.bfloat16(0.0)) for member in range(4)], axis=0
        )
        scores = lax.dot_general(
            stacked, keys[spots, lanes], (((1,), (1,)), ((), ())), preferred_element_type=F32
        )
        seen = mask_ref[band * BAND : (band + 1) * BAND, :]
        raw = jnp.exp(scores).astype(BF16) * jnp.concatenate([seen] * 4, axis=0)
        found = jnp.dot(raw, values[spots, lanes], preferred_element_type=F32)
        found = found / jnp.sum(raw.astype(F32), axis=-1, keepdims=True)
        result = found[:BAND]
        for member in range(1, 4):
            result = jnp.where(head == member, found[member * BAND : (member + 1) * BAND], result)
        out_ref[cells, lanes] = result

    def step(f, carry):
        for quad in range(2):
            for band in range(2):
                attend(f, quad, band)
        return carry

    lax.fori_loop(0, FRAMES_DEV, step, 0)


def far_part(keep_ref, rows_ref, out_ref, weights, queries, keys, values, ones):
    block, every = rows_ref[...], slice(0, FAR_ROWS)
    scaled_heads(block, weights, 0, ones, queries, every, HEAD_DIM**-0.5)
    scaled_heads(block, weights, 1, ones, keys, every, 1.0)
    values[every, :] = jnp.dot(block, weights[:, 2 * HALF :], preferred_element_type=F32).astype(BF16)
    kept = [jnp.where(keep_ref[g] == 1, 1.0, 0.0).astype(F32) for g in range(FRAMES)]
    for quad in range(2):
        lanes = slice(quad * QUAD, (quad + 1) * QUAD)
        for f in range(FRAMES):
            query = queries[f * QUARTER : (f + 1) * QUARTER, lanes]
            products = [query * keys[g * QUARTER : (g + 1) * QUARTER, lanes] for g in range(f + 1)]
            scores = jnp.dot(jnp.concatenate(products, axis=0), ones, preferred_element_type=F32)
            raw = jnp.exp(scores)
            total = raw[f * QUARTER :, :]
            mixed = total * values[f * QUARTER : (f + 1) * QUARTER, lanes].astype(F32)
            for g in range(f):
                weight = raw[g * QUARTER : (g + 1) * QUARTER, :] * kept[g]
                total += weight
                mixed += weight * values[g * QUARTER : (g + 1) * QUARTER, lanes].astype(F32)
            out_ref[f * QUARTER : (f + 1) * QUARTER, lanes] = (mixed / total).astype(BF16)


def near_kernel(near_rows, mask_ref, weights, near_out, queries, keys, values):
    near_part(near_rows, mask_ref, near_out, weights, queries, keys, values, head_ones())


def far_kernel(keep_ref, far_rows, weights, far_out, queries, keys, values):
    far_part(keep_ref, far_rows, far_out, weights, queries, keys, values, head_ones())


NEAR_SHAPE = jax.ShapeDtypeStruct((OWN_ROWS, HALF), F32)
FAR_SHAPE = jax.ShapeDtypeStruct((FAR_ROWS, HALF), BF16)


def half_call(kernel, shapes, scalars, arrays, key_rows, flops, name):
    whole = pl.BlockSpec(memory_space=pltpu.VMEM)
    return pl.pallas_call(
        kernel,
        out_shape=shapes,
        in_specs=[pl.BlockSpec(memory_space=pltpu.SMEM)] * len(scalars)
        + [whole] * len(arrays),
        out_specs=[whole] * len(shapes),
        scratch_shapes=[
            pltpu.VMEM((OWN_ROWS, HALF), BF16),
            pltpu.VMEM((key_rows, HALF), BF16),
            pltpu.VMEM((key_rows, HALF), BF16),
        ],
        compiler_params=pltpu.CompilerParams(vmem_limit_bytes=VMEM),
        cost_estimate=pl.CostEstimate(flops=flops, bytes_accessed=7 * 10**6, transcendentals=10**6),
        name=name,
    )(*scalars, *arrays)


def out_kernel(
    place_ref, coef_ref, near_a, near_b, f0, f1, f2, f3, weight_a, weight_b, state_ref, noise_ref, out_ref, mixed
):
    frame = place_ref[0]
    core = lax.rem(frame, 2)
    lanes_a = pl.ds(pl.multiple_of(core * HALF, HALF), HALF)
    lanes_b = pl.ds(pl.multiple_of((1 - core) * HALF, HALF), HALF)
    for hop, piece in enumerate((f0, f1, f2, f3)):
        source = lax.rem(frame + 4 - hop, 4)
        for f in range(FRAMES_DEV):
            cells = pl.ds(pl.multiple_of(f * CELLS + source * QUARTER, QUARTER), QUARTER)
            arrived = slice(f * QUARTER, (f + 1) * QUARTER)
            first, second = piece[arrived, :HALF], piece[arrived, HALF:]
            if hop % 2 == 1:
                first, second = second, first
            mixed[cells, lanes_a] = (near_a[cells, :] + first.astype(F32)).astype(BF16)
            mixed[cells, lanes_b] = (near_b[cells, :] + second.astype(F32)).astype(BF16)
    for f in range(FRAMES_DEV):
        rows = slice(f * CELLS, (f + 1) * CELLS)
        for lanes, weight in ((lanes_a, weight_a), (lanes_b, weight_b)):
            update = jnp.dot(mixed[rows, :], weight[...], preferred_element_type=F32)
            out_ref[rows, lanes] = (
                state_ref[rows, lanes].astype(F32)
                + coef_ref[0, f] * update
                + coef_ref[1, f] * noise_ref[rows, lanes].astype(F32)
            ).astype(BF16)


def finish(place_ids, coefs, near_a, near_b, far, weight_a, weight_b, state, noise):
    whole = pl.BlockSpec(memory_space=pltpu.VMEM)
    scalar = pl.BlockSpec(memory_space=pltpu.SMEM)
    return pl.pallas_call(
        out_kernel,
        out_shape=jax.ShapeDtypeStruct((OWN_ROWS, WIDTH), BF16),
        in_specs=[scalar, scalar] + [whole] * 10,
        out_specs=whole,
        scratch_shapes=[pltpu.VMEM((OWN_ROWS, WIDTH), BF16)],
        compiler_params=pltpu.CompilerParams(vmem_limit_bytes=VMEM),
        cost_estimate=pl.CostEstimate(flops=2 * 10**9, bytes_accessed=7 * 10**6, transcendentals=0),
        name="out",
    )(place_ids, coefs, near_a, near_b, *far, weight_a, weight_b, state, noise)


def sigma_of(levels):
    return SIGMA_TOP * jnp.exp(levels.astype(F32) * LOG_DECAY)


def body(latent_state, noise_draws, step_index, keep_frame, qkv_weight, out_weight):
    frame = lax.axis_index("frame")
    lat = lax.axis_index("lat")
    x = lax.axis_index("lon")
    core, z_lo = frame % 2, frame // 2
    z_hi, y = lat // 4, lat % 4

    def arranged(*spots):
        return jnp.stack([jnp.asarray(spot, jnp.int32) % 4 for spot in spots])

    state = latent_state.reshape(OWN_ROWS, WIDTH)
    place_ids = frame.reshape(1).astype(jnp.int32)
    columns = [lax.dynamic_slice(qkv_weight, (0, s * WIDTH + core * HALF), (16, HALF)) for s in range(3)]
    columns.append(lax.dynamic_slice(out_weight, (0, core * HALF), (16, HALF)))
    own_rows = jnp.concatenate(columns, axis=1)
    z_in = [lax.ppermute(own_rows, EVERY, z_routes(slot)) for slot in (1, 2, 3)]
    z_in = [own_rows, *z_in]
    side = 2 * z_lo - 1
    (z_rows,) = place_rows(
        1, arranged(z_hi, z_hi + side, z_hi - side, z_hi + 2), z_in, [(4, 16, 4 * HALF)]
    )
    plane_in = [z_rows] + [lax.ppermute(z_rows, EVERY, plane_routes(2, hop)) for hop in (1, 2, 3)]
    up, down = latent_state[:, ROWS - REACH :], latent_state[:, :REACH]
    up, down, plane_in[1] = lax.optimization_barrier((up, down, plane_in[1]))
    top = lax.ppermute(up, "lat", [(i, i + 1) for i in range(15)])
    bottom = lax.ppermute(down, "lat", [(i + 1, i) for i in range(15)])
    inner, outer = jnp.where(core == 0, y, x), jnp.where(core == 0, x, y)
    plane, plane_out = place_rows(
        2, arranged(inner, inner - 1, inner - 2, inner - 3), plane_in,
        [(4, 4, 16, 3 * HALF), (4, 4, 16, HALF)],
    )
    outer_spots = arranged(outer, outer - 1, outer - 2, outer - 3, core)
    last_in = [plane] + [lax.ppermute(plane, EVERY, plane_routes(3, hop)) for hop in (1, 2, 3)]
    quarters = latent_state.reshape(FRAMES_DEV, 4, QUARTER, WIDTH)

    def quarter(index):
        taken = lax.dynamic_index_in_dim(quarters, index % 4, axis=1, keepdims=False)
        return taken.reshape(FRAMES_DEV * QUARTER, WIDTH)

    sent = [quarter(frame + hop) for hop in (1, 2, 3)]
    *sent, top, bottom = lax.optimization_barrier((*sent, top, bottom))
    far_in = [quarter(frame)] + [lax.ppermute(sent[hop - 1], "frame", frame_routes(hop)) for hop in (1, 2, 3)]
    far_rows = prepare_far(place_ids, far_in)
    *last_in, far_rows, mask, top, bottom = lax.optimization_barrier(
        (*last_in, far_rows, near_mask(lat), top, bottom)
    )
    east, west = edges_of(latent_state, top, bottom)
    *last_in, east, west = lax.optimization_barrier((*last_in, east, west))
    left = lax.ppermute(east, "lon", [(i, (i + 1) % 4) for i in range(4)])
    right = lax.ppermute(west, "lon", [((i + 1) % 4, i) for i in range(4)])
    (weight_a,) = place_rows(3, outer_spots, last_in, [(4, 4, 4, 16, 3 * HALF)])
    weight_a = weight_a.reshape(WIDTH, 3 * HALF)
    weight_b = lax.ppermute(weight_a, EVERY, core_routes())

    (far_a,) = half_call(
        far_kernel, [FAR_SHAPE], [keep_frame], [far_rows, weight_a], FAR_ROWS, 3 * 10**9, "far"
    )
    (far_b,) = half_call(
        far_kernel, [FAR_SHAPE], [keep_frame], [far_rows, weight_b], FAR_ROWS, 3 * 10**9, "far"
    )
    far_out = jnp.concatenate([far_a, far_b], axis=1).reshape(4, FRAMES_DEV * QUARTER, WIDTH)

    def frames_of(index):
        return lax.dynamic_index_in_dim(far_out, index % 4, axis=0, keepdims=False)

    far_back = [frames_of(frame)] + [
        lax.ppermute(frames_of(frame + hop), "frame", frame_routes(hop)) for hop in (1, 2, 3)
    ]
    left, right, *far_back = lax.optimization_barrier((left, right, *far_back))
    near_rows = prepare(state, top.reshape(-1, WIDTH), bottom.reshape(-1, WIDTH), left, right)
    plane_out, near_rows = lax.optimization_barrier((plane_out, near_rows))
    (near_a,) = half_call(
        near_kernel, [NEAR_SHAPE], [], [near_rows, mask, weight_a], NEAR_ROWS, 8 * 10**9, "near"
    )
    out_in = [plane_out] + [lax.ppermute(plane_out, EVERY, plane_routes(3, hop)) for hop in (1, 2, 3)]
    *out_in, near_a = lax.optimization_barrier((*out_in, near_a))
    (out_a,) = place_rows(3, outer_spots, out_in, [(4, 4, 4, 16, HALF)])
    out_a = out_a.reshape(WIDTH, HALF)
    out_b = lax.ppermute(out_a, EVERY, core_routes())
    (near_b,) = half_call(
        near_kernel, [NEAR_SHAPE], [], [near_rows, mask, weight_b], NEAR_ROWS, 8 * 10**9, "near"
    )

    noise_now = sigma_of(step_index)
    noise_next = sigma_of(step_index + 1)
    spread = NOISE_SHARE * jnp.sqrt(noise_now * noise_now - noise_next * noise_next)
    coefs = jnp.stack([noise_next - noise_now, spread])
    denoised = finish(
        place_ids, coefs, near_a, near_b, far_back, out_a, out_b, state, noise_draws.reshape(OWN_ROWS, WIDTH)
    )
    return denoised.reshape(latent_state.shape)


def solution(mesh):
    return jax.shard_map(
        body,
        mesh=mesh,
        in_specs=(
            P("frame", "lat", "lon", None),
            P(None, "frame", "lat", "lon", None),
            P("frame"),
            P(),
            P(("lat", "lon"), None),
            P(("lat", "lon"), None),
        ),
        out_specs=P("frame", "lat", "lon", None),
        check_vma=False,
    )
```

```python
import functools
import math

import jax
import jax.numpy as jnp
from jax import lax
from jax.experimental import pallas as pl
from jax.experimental.pallas import tpu as pltpu
from jax.sharding import PartitionSpec as P

HEAD_DIM = 64
REACH = 6
SIDE = 2 * REACH
SIGMA_TOP = 4.0
LOG_DECAY = math.log(0.8)
NOISE_SHARE = 0.5

FRAMES_DEV = 2
ROWS = 12
COLS = 16
CELLS = ROWS * COLS
WIDTH = 1024
TOTAL_ROWS = 192
FRAMES = 8
QUARTER = CELLS // 4
HALF = WIDTH // 2
QUAD = 256
MID = 176
LOW = MID + ROWS * (COLS + SIDE)
KEYS = LOW + 176
BAND = CELLS // 2
BAND_SKIP = MID
BAND_KEYS = LOW
NEAR_ROWS = FRAMES_DEV * KEYS
FAR_ROWS = FRAMES * QUARTER
OWN_ROWS = FRAMES_DEV * CELLS
VMEM = 32 * 1024 * 1024
BF16 = jnp.bfloat16
F32 = jnp.float32
EVERY = ("frame", "lat", "lon")


def place(z_lo, core, z_hi, y, x):
    return ((z_lo * 2 + core) * 16 + (z_hi % 4) * 4 + y % 4) * 4 + x % 4


def all_places():
    return [
        (z_lo, core, z_hi, y, x)
        for z_lo in range(2)
        for core in range(2)
        for z_hi in range(4)
        for y in range(4)
        for x in range(4)
    ]


def z_routes(slot):
    pairs = []
    for z_lo, core, z_hi, y, x in all_places():
        if slot == 1:
            source = (1 - z_lo, core, z_hi - 1 if z_lo == 0 else z_hi + 1, y, x)
        elif slot == 2:
            source = (z_lo, core, z_hi + 1 if z_lo == 0 else z_hi - 1, y, x)
        else:
            source = (1 - z_lo, core, z_hi + 2, y, x)
        pairs.append((place(*source), place(z_lo, core, z_hi, y, x)))
    return pairs


def plane_routes(stage, hop):
    pairs = []
    for z_lo, core, z_hi, y, x in all_places():
        along_y = (core == 0) == (stage == 2)
        target = (z_lo, core, z_hi, y + hop, x) if along_y else (z_lo, core, z_hi, y, x + hop)
        pairs.append((place(z_lo, core, z_hi, y, x), place(*target)))
    return pairs


def core_routes():
    return [(place(zl, c, zh, y, x), place(zl, 1 - c, zh, y, x)) for zl, c, zh, y, x in all_places()]


def frame_routes(hop):
    return [(p, (p + hop) % 4) for p in range(4)]


def place_kernel(mode, spots_ref, *refs):
    arrived, targets = refs[:4], refs[4:]
    split = 3 * HALF

    def run(by_first):
        for d in range(4):
            spot = spots_ref[d]
            if mode == 1:
                targets[0][spot] = arrived[d][...]
                continue

            def step(z, carry, d=d, spot=spot):
                if mode == 2:
                    targets[0][z, spot] = arrived[d][z, :, :split]
                    targets[1][z, spot] = arrived[d][z, :, split:]
                elif by_first:
                    targets[0][z, spot] = arrived[d][z]
                else:
                    targets[0][z, :, spot] = arrived[d][z]
                return carry

            lax.fori_loop(0, 4, step, 0)

    if mode < 3:
        run(False)
    else:
        pl.when(spots_ref[4] == 0)(lambda: run(False))
        pl.when(spots_ref[4] == 1)(lambda: run(True))


def place_rows(mode, spots, arrived, shapes):
    whole = pl.BlockSpec(memory_space=pltpu.VMEM)
    size = sum(2 * math.prod(shape) for shape in shapes)
    return pl.pallas_call(
        functools.partial(place_kernel, mode),
        out_shape=[jax.ShapeDtypeStruct(shape, BF16) for shape in shapes],
        in_specs=[pl.BlockSpec(memory_space=pltpu.SMEM)] + [whole] * 4,
        out_specs=[whole] * len(shapes),
        compiler_params=pltpu.CompilerParams(vmem_limit_bytes=VMEM),
        cost_estimate=pl.CostEstimate(flops=0, bytes_accessed=2 * size, transcendentals=0),
        name="place",
    )(spots, *arrived)


def near_mask(lat):
    spot = jnp.arange(BAND_KEYS, dtype=jnp.int32)[None, :]
    cell = jnp.arange(CELLS, dtype=jnp.int32)[:, None]
    spot = spot + jnp.where(cell < CELLS // 2, 0, BAND_SKIP)
    part = jnp.where(spot < MID, 0, jnp.where(spot < LOW, 1, 2))
    base = jnp.where(part == 0, 0, jnp.where(part == 1, MID, LOW))
    first_row = jnp.where(part == 0, 0, jnp.where(part == 1, REACH, REACH + ROWS))
    tall = jnp.where(part == 1, ROWS, REACH)
    local = spot - base
    centre = tall * COLS
    edge = tall * REACH
    side = local - centre
    right = side >= edge
    side = jnp.where(right, side - edge, side)
    inner = local < centre
    key_row = first_row + jnp.where(inner, local // COLS, side // REACH)
    key_col = jnp.where(
        inner, REACH + local % COLS, jnp.where(right, COLS + REACH, 0) + side % REACH
    )
    lat_gap = key_row - cell // COLS
    lon_gap = key_col - cell % COLS
    global_row = lat * ROWS + key_row - REACH
    inside = (global_row >= 0) & (global_row < TOTAL_ROWS) & (local < centre + 2 * edge)
    seen = (lat_gap >= 0) & (lat_gap <= SIDE) & (lon_gap >= 0) & (lon_gap <= SIDE)
    return (seen & inside).astype(BF16)


def edge_kernel(own, top, bottom, east, west, east_tmp, west_tmp):
    for f in range(FRAMES_DEV):
        for row in range(ROWS + SIDE):
            if row < REACH:
                block = top[f, row]
            elif row < REACH + ROWS:
                block = own[f, row - REACH]
            else:
                block = bottom[f, row - REACH - ROWS]
            block = block.astype(F32)
            start = (f * (ROWS + SIDE) + row) * REACH
            east_tmp[start : start + REACH, :] = block[COLS - REACH :]
            west_tmp[start : start + REACH, :] = block[:REACH]
    east[...] = east_tmp[...].astype(BF16)
    west[...] = west_tmp[...].astype(BF16)


def edges_of(own, top, bottom):
    whole = pl.BlockSpec(memory_space=pltpu.VMEM)
    rows = FRAMES_DEV * (ROWS + SIDE) * REACH
    return pl.pallas_call(
        edge_kernel,
        out_shape=[jax.ShapeDtypeStruct((rows, WIDTH), BF16)] * 2,
        in_specs=[whole] * 3,
        out_specs=[whole] * 2,
        scratch_shapes=[pltpu.VMEM((rows, WIDTH), F32)] * 2,
        compiler_params=pltpu.CompilerParams(vmem_limit_bytes=VMEM),
        cost_estimate=pl.CostEstimate(flops=10**6, bytes_accessed=3 * 10**6, transcendentals=0),
        name="edges",
    )(own, top, bottom)


def normed(block):
    rows = block.astype(F32)
    return rows * lax.rsqrt(jnp.mean(rows * rows, axis=-1, keepdims=True) + 1e-05)


def prep_kernel(own, top, bottom, left, right, near_out, rows_tmp, edge_tmp):
    def place_rows(source, start, offset, count):
        def step(index, carry):
            taken = source[pl.ds(pl.multiple_of(start + index * 48, 16), 48), :]
            rows_tmp[pl.ds(pl.multiple_of(offset + index * 48, 16), 48), :] = normed(taken)
            return carry

        lax.fori_loop(0, count // 48, step, 0)

    for f in range(FRAMES_DEV):
        base = f * KEYS
        place_rows(own, f * CELLS, base + MID, CELLS)
        place_rows(top, f * 96, base, 96)
        place_rows(bottom, f * 96, base + LOW, 96)
        rows_tmp[base + MID - 8 : base + MID, :] = jnp.zeros((8, WIDTH), F32)
        rows_tmp[base + KEYS - 8 : base + KEYS, :] = jnp.zeros((8, WIDTH), F32)
    for index, edge in enumerate((left, right)):
        for chunk in range(6):
            spot = slice(chunk * 48, (chunk + 1) * 48)
            edge_tmp[spot, :] = normed(edge[spot, :])
        for f in range(FRAMES_DEV):
            for first, count, target in (
                (0, 36, 96 + index * 36),
                (36, 72, MID + CELLS + index * 72),
                (108, 36, LOW + 96 + index * 36),
            ):
                start = f * 144 + first
                rows_tmp[f * KEYS + target : f * KEYS + target + count, :] = edge_tmp[start : start + count, :]

    def settle(index, carry):
        rows = pl.ds(pl.multiple_of(index * 32, 32), 32)
        near_out[rows, :] = rows_tmp[rows, :].astype(BF16)
        return carry

    lax.fori_loop(0, NEAR_ROWS // 32, settle, 0)

def far_prep_kernel(frame_ref, f0, f1, f2, f3, far_out):
    for hop, piece in enumerate((f0, f1, f2, f3)):
        source = lax.rem(frame_ref[0] + 4 - hop, 4)

        def far_step(index, carry, piece=piece, source=source):
            taken = piece[pl.ds(pl.multiple_of(index * 48, 16), 48), :]
            target = pl.ds(pl.multiple_of(source * (2 * QUARTER) + index * 48, 16), 48)
            far_out[target, :] = normed(taken).astype(BF16)
            return carry

        lax.fori_loop(0, 2, far_step, 0)


def prepare_far(frame, far):
    whole = pl.BlockSpec(memory_space=pltpu.VMEM)
    return pl.pallas_call(
        far_prep_kernel,
        out_shape=jax.ShapeDtypeStruct((FAR_ROWS, WIDTH), BF16),
        in_specs=[pl.BlockSpec(memory_space=pltpu.SMEM)] + [whole] * 4,
        out_specs=whole,
        compiler_params=pltpu.CompilerParams(vmem_limit_bytes=VMEM),
        cost_estimate=pl.CostEstimate(flops=10**8, bytes_accessed=16 * 10**5, transcendentals=0),
        name="prep_far",
    )(frame, *far)


def prepare(own, top, bottom, left, right):
    whole = pl.BlockSpec(memory_space=pltpu.VMEM)
    return pl.pallas_call(
        prep_kernel,
        out_shape=jax.ShapeDtypeStruct((NEAR_ROWS, WIDTH), BF16),
        in_specs=[whole] * 5,
        out_specs=whole,
        scratch_shapes=[pltpu.VMEM((NEAR_ROWS, WIDTH), F32), pltpu.VMEM((288, WIDTH), F32)],
        compiler_params=pltpu.CompilerParams(vmem_limit_bytes=VMEM),
        cost_estimate=pl.CostEstimate(flops=10**9, bytes_accessed=8 * 10**6, transcendentals=0),
        name="prep",
    )(own, top, bottom, left, right)


def head_ones():
    row = lax.broadcasted_iota(jnp.int32, (QUAD, QUAD), 0) // HEAD_DIM
    col = lax.broadcasted_iota(jnp.int32, (QUAD, QUAD), 1) // HEAD_DIM
    return jnp.where(row == col, 1.0, 0.0).astype(BF16)


def head_scale(values, ones):
    squares = jnp.dot((values * values).astype(BF16), ones, preferred_element_type=F32)
    return values * lax.rsqrt(squares * (1.0 / HEAD_DIM) + 1e-06)


def scaled_heads(rows, weights, part, ones, target, spot, factor):
    found = jnp.dot(rows, weights[:, part * HALF : (part + 1) * HALF], preferred_element_type=F32)
    for quad in range(2):
        lanes = slice(quad * QUAD, (quad + 1) * QUAD)
        target[spot, lanes] = head_scale(found[:, lanes], ones).astype(BF16) * jnp.bfloat16(factor)


def near_part(rows_ref, mask_ref, out_ref, weights, queries, keys, values, ones):
    def key_step(index, carry):
        spot = pl.ds(pl.multiple_of(index * KEYS, 16), KEYS)
        block = rows_ref[spot, :]
        scaled_heads(block, weights, 1, ones, keys, spot, 1.0)
        values[spot, :] = jnp.dot(block, weights[:, 2 * HALF :], preferred_element_type=F32).astype(BF16)
        cells = rows_ref[pl.ds(pl.multiple_of(index * KEYS + MID, 16), CELLS), :]
        target = pl.ds(pl.multiple_of(index * CELLS, CELLS), CELLS)
        scaled_heads(cells, weights, 0, ones, queries, target, HEAD_DIM**-0.5)
        return carry

    lax.fori_loop(0, FRAMES_DEV, key_step, 0)

    head = lax.broadcasted_iota(jnp.int32, (BAND, QUAD), 1) // HEAD_DIM

    def attend(f, quad, band):
        lanes = slice(quad * QUAD, (quad + 1) * QUAD)
        cells = pl.ds(pl.multiple_of(f * CELLS + band * BAND, BAND), BAND)
        spots = pl.ds(pl.multiple_of(f * KEYS + band * BAND_SKIP, 16), BAND_KEYS)
        query = queries[cells, lanes]
        stacked = jnp.concatenate(
            [jnp.where(head == member, query, jnp.bfloat16(0.0)) for member in range(4)], axis=0
        )
        scores = lax.dot_general(
            stacked, keys[spots, lanes], (((1,), (1,)), ((), ())), preferred_element_type=F32
        )
        seen = mask_ref[band * BAND : (band + 1) * BAND, :]
        raw = jnp.exp(scores).astype(BF16) * jnp.concatenate([seen] * 4, axis=0)
        found = jnp.dot(raw, values[spots, lanes], preferred_element_type=F32)
        found = found / jnp.sum(raw.astype(F32), axis=-1, keepdims=True)
        result = found[:BAND]
        for member in range(1, 4):
            result = jnp.where(head == member, found[member * BAND : (member + 1) * BAND], result)
        out_ref[cells, lanes] = result

    def step(f, carry):
        for quad in range(2):
            for band in range(2):
                attend(f, quad, band)
        return carry

    lax.fori_loop(0, FRAMES_DEV, step, 0)


def far_part(keep_ref, rows_ref, out_ref, weights, queries, keys, values, ones):
    block, every = rows_ref[...], slice(0, FAR_ROWS)
    scaled_heads(block, weights, 0, ones, queries, every, HEAD_DIM**-0.5)
    scaled_heads(block, weights, 1, ones, keys, every, 1.0)
    values[every, :] = jnp.dot(block, weights[:, 2 * HALF :], preferred_element_type=F32).astype(BF16)
    kept = [jnp.where(keep_ref[g] == 1, 1.0, 0.0).astype(F32) for g in range(FRAMES)]
    for quad in range(2):
        lanes = slice(quad * QUAD, (quad + 1) * QUAD)
        for f in range(FRAMES):
            query = queries[f * QUARTER : (f + 1) * QUARTER, lanes]
            products = [query * keys[g * QUARTER : (g + 1) * QUARTER, lanes] for g in range(f + 1)]
            scores = jnp.dot(jnp.concatenate(products, axis=0), ones, preferred_element_type=F32)
            raw = jnp.exp(scores)
            total = raw[f * QUARTER :, :]
            mixed = total * values[f * QUARTER : (f + 1) * QUARTER, lanes].astype(F32)
            for g in range(f):
                weight = raw[g * QUARTER : (g + 1) * QUARTER, :] * kept[g]
                total += weight
                mixed += weight * values[g * QUARTER : (g + 1) * QUARTER, lanes].astype(F32)
            out_ref[f * QUARTER : (f + 1) * QUARTER, lanes] = (mixed / total).astype(BF16)


def near_kernel(near_rows, mask_ref, weights, near_out, queries, keys, values):
    near_part(near_rows, mask_ref, near_out, weights, queries, keys, values, head_ones())


def far_kernel(keep_ref, far_rows, weights, far_out, queries, keys, values):
    far_part(keep_ref, far_rows, far_out, weights, queries, keys, values, head_ones())


NEAR_SHAPE = jax.ShapeDtypeStruct((OWN_ROWS, HALF), F32)
FAR_SHAPE = jax.ShapeDtypeStruct((FAR_ROWS, HALF), BF16)


def half_call(kernel, shapes, scalars, arrays, key_rows, flops, name):
    whole = pl.BlockSpec(memory_space=pltpu.VMEM)
    return pl.pallas_call(
        kernel,
        out_shape=shapes,
        in_specs=[pl.BlockSpec(memory_space=pltpu.SMEM)] * len(scalars)
        + [whole] * len(arrays),
        out_specs=[whole] * len(shapes),
        scratch_shapes=[
            pltpu.VMEM((OWN_ROWS, HALF), BF16),
            pltpu.VMEM((key_rows, HALF), BF16),
            pltpu.VMEM((key_rows, HALF), BF16),
        ],
        compiler_params=pltpu.CompilerParams(vmem_limit_bytes=VMEM),
        cost_estimate=pl.CostEstimate(flops=flops, bytes_accessed=7 * 10**6, transcendentals=10**6),
        name=name,
    )(*scalars, *arrays)


def out_kernel(
    place_ref, coef_ref, near_a, near_b, f0, f1, f2, f3, weight_a, weight_b, state_ref, noise_ref, out_ref, mixed
):
    frame = place_ref[0]
    core = lax.rem(frame, 2)
    lanes_a = pl.ds(pl.multiple_of(core * HALF, HALF), HALF)
    lanes_b = pl.ds(pl.multiple_of((1 - core) * HALF, HALF), HALF)
    for hop, piece in enumerate((f0, f1, f2, f3)):
        source = lax.rem(frame + 4 - hop, 4)
        for f in range(FRAMES_DEV):
            cells = pl.ds(pl.multiple_of(f * CELLS + source * QUARTER, QUARTER), QUARTER)
            arrived = slice(f * QUARTER, (f + 1) * QUARTER)
            first, second = piece[arrived, :HALF], piece[arrived, HALF:]
            if hop % 2 == 1:
                first, second = second, first
            mixed[cells, lanes_a] = (near_a[cells, :] + first.astype(F32)).astype(BF16)
            mixed[cells, lanes_b] = (near_b[cells, :] + second.astype(F32)).astype(BF16)
    for f in range(FRAMES_DEV):
        rows = slice(f * CELLS, (f + 1) * CELLS)
        for lanes, weight in ((lanes_a, weight_a), (lanes_b, weight_b)):
            update = jnp.dot(mixed[rows, :], weight[...], preferred_element_type=F32)
            out_ref[rows, lanes] = (
                state_ref[rows, lanes].astype(F32)
                + coef_ref[0, f] * update
                + coef_ref[1, f] * noise_ref[rows, lanes].astype(F32)
            ).astype(BF16)


def finish(place_ids, coefs, near_a, near_b, far, weight_a, weight_b, state, noise):
    whole = pl.BlockSpec(memory_space=pltpu.VMEM)
    scalar = pl.BlockSpec(memory_space=pltpu.SMEM)
    return pl.pallas_call(
        out_kernel,
        out_shape=jax.ShapeDtypeStruct((OWN_ROWS, WIDTH), BF16),
        in_specs=[scalar, scalar] + [whole] * 10,
        out_specs=whole,
        scratch_shapes=[pltpu.VMEM((OWN_ROWS, WIDTH), BF16)],
        compiler_params=pltpu.CompilerParams(vmem_limit_bytes=VMEM),
        cost_estimate=pl.CostEstimate(flops=2 * 10**9, bytes_accessed=7 * 10**6, transcendentals=0),
        name="out",
    )(place_ids, coefs, near_a, near_b, *far, weight_a, weight_b, state, noise)


def sigma_of(levels):
    return SIGMA_TOP * jnp.exp(levels.astype(F32) * LOG_DECAY)


def body(latent_state, noise_draws, step_index, keep_frame, qkv_weight, out_weight):
    frame = lax.axis_index("frame")
    lat = lax.axis_index("lat")
    x = lax.axis_index("lon")
    core, z_lo = frame % 2, frame // 2
    z_hi, y = lat // 4, lat % 4

    def arranged(*spots):
        return jnp.stack([jnp.asarray(spot, jnp.int32) % 4 for spot in spots])

    state = latent_state.reshape(OWN_ROWS, WIDTH)
    place_ids = frame.reshape(1).astype(jnp.int32)
    columns = [lax.dynamic_slice(qkv_weight, (0, s * WIDTH + core * HALF), (16, HALF)) for s in range(3)]
    columns.append(lax.dynamic_slice(out_weight, (0, core * HALF), (16, HALF)))
    own_rows = jnp.concatenate(columns, axis=1)
    z_in = [lax.ppermute(own_rows, EVERY, z_routes(slot)) for slot in (1, 2, 3)]
    z_in = [own_rows, *z_in]
    side = 2 * z_lo - 1
    (z_rows,) = place_rows(
        1, arranged(z_hi, z_hi + side, z_hi - side, z_hi + 2), z_in, [(4, 16, 4 * HALF)]
    )
    plane_in = [z_rows] + [lax.ppermute(z_rows, EVERY, plane_routes(2, hop)) for hop in (1, 2, 3)]
    up, down = latent_state[:, ROWS - REACH :], latent_state[:, :REACH]
    up, down, plane_in[1] = lax.optimization_barrier((up, down, plane_in[1]))
    top = lax.ppermute(up, "lat", [(i, i + 1) for i in range(15)])
    bottom = lax.ppermute(down, "lat", [(i + 1, i) for i in range(15)])
    inner, outer = jnp.where(core == 0, y, x), jnp.where(core == 0, x, y)
    plane, plane_out = place_rows(
        2, arranged(inner, inner - 1, inner - 2, inner - 3), plane_in,
        [(4, 4, 16, 3 * HALF), (4, 4, 16, HALF)],
    )
    outer_spots = arranged(outer, outer - 1, outer - 2, outer - 3, core)
    last_in = [plane] + [lax.ppermute(plane, EVERY, plane_routes(3, hop)) for hop in (1, 2, 3)]
    quarters = latent_state.reshape(FRAMES_DEV, 4, QUARTER, WIDTH)

    def quarter(index):
        taken = lax.dynamic_index_in_dim(quarters, index % 4, axis=1, keepdims=False)
        return taken.reshape(FRAMES_DEV * QUARTER, WIDTH)

    sent = [quarter(frame + hop) for hop in (1, 2, 3)]
    *sent, top, bottom = lax.optimization_barrier((*sent, top, bottom))
    far_in = [quarter(frame)] + [lax.ppermute(sent[hop - 1], "frame", frame_routes(hop)) for hop in (1, 2, 3)]
    far_rows = prepare_far(place_ids, far_in)
    *last_in, far_rows, mask, top, bottom = lax.optimization_barrier(
        (*last_in, far_rows, near_mask(lat), top, bottom)
    )
    east, west = edges_of(latent_state, top, bottom)
    *last_in, east, west = lax.optimization_barrier((*last_in, east, west))
    left = lax.ppermute(east, "lon", [(i, (i + 1) % 4) for i in range(4)])
    right = lax.ppermute(west, "lon", [((i + 1) % 4, i) for i in range(4)])
    (weight_a,) = place_rows(3, outer_spots, last_in, [(4, 4, 4, 16, 3 * HALF)])
    weight_a = weight_a.reshape(WIDTH, 3 * HALF)
    weight_b = lax.ppermute(weight_a, EVERY, core_routes())

    (far_a,) = half_call(
        far_kernel, [FAR_SHAPE], [keep_frame], [far_rows, weight_a], FAR_ROWS, 3 * 10**9, "far"
    )
    (far_b,) = half_call(
        far_kernel, [FAR_SHAPE], [keep_frame], [far_rows, weight_b], FAR_ROWS, 3 * 10**9, "far"
    )
    far_out = jnp.concatenate([far_a, far_b], axis=1).reshape(4, FRAMES_DEV * QUARTER, WIDTH)

    def frames_of(index):
        return lax.dynamic_index_in_dim(far_out, index % 4, axis=0, keepdims=False)

    far_back = [frames_of(frame)] + [
        lax.ppermute(frames_of(frame + hop), "frame", frame_routes(hop)) for hop in (1, 2, 3)
    ]
    left, right, plane_out, *far_back = lax.optimization_barrier((left, right, plane_out, *far_back))
    near_rows = prepare(state, top.reshape(-1, WIDTH), bottom.reshape(-1, WIDTH), left, right)
    (near_a,) = half_call(
        near_kernel, [NEAR_SHAPE], [], [near_rows, mask, weight_a], NEAR_ROWS, 10**9, "near"
    )
    out_in = [plane_out] + [lax.ppermute(plane_out, EVERY, plane_routes(3, hop)) for hop in (1, 2, 3)]
    *out_in, near_a = lax.optimization_barrier((*out_in, near_a))
    (out_a,) = place_rows(3, outer_spots, out_in, [(4, 4, 4, 16, HALF)])
    out_a = out_a.reshape(WIDTH, HALF)
    out_b = lax.ppermute(out_a, EVERY, core_routes())
    (near_b,) = half_call(
        near_kernel, [NEAR_SHAPE], [], [near_rows, mask, weight_b], NEAR_ROWS, 8 * 10**9, "near"
    )

    noise_now = sigma_of(step_index)
    noise_next = sigma_of(step_index + 1)
    spread = NOISE_SHARE * jnp.sqrt(noise_now * noise_now - noise_next * noise_next)
    coefs = jnp.stack([noise_next - noise_now, spread])
    denoised = finish(
        place_ids, coefs, near_a, near_b, far_back, out_a, out_b, state, noise_draws.reshape(OWN_ROWS, WIDTH)
    )
    return denoised.reshape(latent_state.shape)


def solution(mesh):
    return jax.shard_map(
        body,
        mesh=mesh,
        in_specs=(
            P("frame", "lat", "lon", None),
            P(None, "frame", "lat", "lon", None),
            P("frame"),
            P(),
            P(("lat", "lon"), None),
            P(("lat", "lon"), None),
        ),
        out_specs=P("frame", "lat", "lon", None),
        check_vma=False,
    )
```
